32 devices in a mesh: blk: 8 (over z, y), rep: 4 (over x, core).
Axes of the slice: x: 2, y: 2, z: 4, core: 2. Of those that a mesh axis runs over, the one named last changes fastest.
Arguments:
- tile_vals: bfloat16 [8, 8, 20, 128, 128], P('blk', 'rep'), may hold values from -4 to 4
- tile_coords: int32 [8, 8, 20, 2], P('blk', 'rep'), may hold values from 0 to 3
- tile_live: int32 [8, 8, 20], P('blk', 'rep'), may hold values from 0 to 1, as said below
- features: bfloat16 [4096, 256], P('blk'), may hold values from -6 to 6
- degree: int32 [4096], P(('blk', 'rep')), may hold values from 512 to 8192
- w_self: bfloat16 [256, 256], replicated, may hold values from -0.375 to 0.375
- w_neigh: bfloat16 [256, 256], replicated, may hold values from -0.375 to 0.375
- cotangent: bfloat16 [4096, 256], P(('blk', 'rep')), may hold values from -6 to 6
Outputs:
- hidden: bfloat16 [4096, 256], P(('blk', 'rep'))
- grad_features: bfloat16 [4096, 256], P(('blk', 'rep'))
- grad_self: float32 [256, 256], replicated
- grad_neigh: float32 [256, 256], replicated
The draws below stay inside these ranges and needn't reach their ends.
Inputs may be any that keep to these rules, and one draw needn't show every extreme that they name: `tile_coords`: entry 0 names a tile row block of the row partition, entry 1 a tile column block of the column partition; tiles with equal coordinates add. `tile_live`: 1 marks a present tile, 0 a padding tile; the share of present tiles differs between row partitions.
All inputs are finite; a program needn't handle non-finite values.
Results may differ from the reference program's by a relative error of at most 0.012.
Values may be sent and summed in bfloat16 or wider, within the bound.
No kernel may reach another device: no remote copies, remote signals or barrier semaphores. Data moves between devices by JAX's collectives and lax.ppermute only.
A program may use at most 64 MiB of HBM per device.

```python
import math
import jax
import jax.numpy as jnp
from jax import lax

D = 256
TILE = 128
ROWS_DEV = 512
BLOCKS_DEV = 4
TILES = 20
PARTITIONS = 8
OFFS = 8
NODES = 4096


def draw_tile_live(key, part):
    rate_key = jax.random.fold_in(key, 17)
    coin_key = jax.random.fold_in(key, 29)
    rates = jax.random.randint(rate_key, (PARTITIONS, 1, 1), 2, 9)
    coins = jax.random.randint(coin_key, (PARTITIONS, OFFS, TILES), 0, 8)
    return (coins < rates).astype(jnp.int32)


def touch_ends(entries, stream_key, low, largest):
    place = [jax.random.randint(jax.random.fold_in(stream_key, axis), (), 0, length) for axis, length in enumerate(entries.shape)]
    longest = entries.shape.index(max(entries.shape))
    beside = place[:longest] + [(place[longest] + 1) % entries.shape[longest]] + place[longest + 1:]
    return entries.at[tuple(place)].set(low).at[tuple(beside)].set(largest)


def block_levels(stream_key, extent, shards, least, largest):
    def one(dim, shards_of):
        draws = jax.random.uniform(jax.random.fold_in(jax.random.fold_in(stream_key, 6), dim), (shards_of,), jnp.float32, least / len(shards), largest / len(shards))
        return jnp.repeat(jnp.exp(draws), extent[dim] // shards_of).reshape((-1,) + (1,) * (len(extent) - dim - 1))

    loudness = one(*shards[0])
    for cut in shards[1:]:
        loudness = loudness * one(*cut)
    return loudness


def centred(rng, extent, deviation, bound, cuts=(), kind=jnp.bfloat16):
    factor_of = block_levels(rng, extent, cuts, -0.22, 0.18) if cuts else 1.0
    drawn = jax.random.normal(rng, extent, jnp.float32) * deviation * factor_of
    return jnp.minimum(jnp.maximum(drawn, -bound), bound).astype(kind)


def setup_inputs(seed: int = 0) -> dict:
    seeds = jax.random.split(jax.random.key(seed), 9)
    return {
        "tile_vals": centred(seeds[0], (PARTITIONS, OFFS, TILES, TILE, TILE), 1.0, 4.0, ((0, 8), (1, 4))),
        "tile_coords": touch_ends(jax.random.randint(seeds[1], (PARTITIONS, OFFS, TILES, 2), 0, BLOCKS_DEV), jax.random.fold_in(seeds[1], 1), 0, BLOCKS_DEV - 1).astype(jnp.int32),
        "tile_live": draw_tile_live(jax.random.fold_in(seeds[8], 71), 0),
        "features": centred(seeds[3], (NODES, D), 1.0, 6.0, ((0, 8),)),
        "degree": touch_ends(jax.random.randint(seeds[4], (NODES,), 512, 8193), jax.random.fold_in(seeds[4], 1), 512, 8192).astype(jnp.int32),
        "w_self": centred(seeds[5], (D, D), D ** -0.5, 0.375),
        "w_neigh": centred(seeds[6], (D, D), D ** -0.5, 0.375),
        "cotangent": centred(seeds[7], (NODES, D), 1.0, 6.0, ((0, 32),)),
    }


def reference(tile_vals, tile_coords, tile_live, features, degree, w_self, w_neigh, cotangent):
    half_span = OFFS // 2
    offset_ids = jnp.arange(OFFS, dtype=jnp.int32)
    block_ids = jnp.arange(BLOCKS_DEV, dtype=jnp.int32)
    panels = features.reshape(PARTITIONS, BLOCKS_DEV, TILE, D)

    def forward_part(row_part):
        col_panels = (row_part + offset_ids - half_span) % PARTITIONS
        source_rows = panels[col_panels[:, None], tile_coords[row_part, :, :, 1]]
        tiles = tile_vals[row_part].astype(jnp.float32) * tile_live[row_part].astype(jnp.float32)[:, :, None, None]
        products = jnp.einsum('qkrc,qkcd->qkrd', tiles, source_rows.astype(jnp.float32))
        onehot = (tile_coords[row_part, :, :, 0][None] == block_ids[:, None, None]).astype(jnp.float32)
        placed = jnp.einsum('iqk,qkrd->ird', onehot, products, precision=lax.Precision.HIGHEST)
        return placed.reshape(ROWS_DEV, D)
    summed = lax.map(forward_part, jnp.arange(PARTITIONS, dtype=jnp.int32)).reshape(NODES, D)
    root_deg = jnp.sqrt(degree.astype(jnp.float32))[:, None]
    aggregate = (summed / root_deg).astype(jnp.bfloat16)
    preact = jnp.dot(features, w_self, preferred_element_type=jnp.float32) + jnp.dot(aggregate, w_neigh, preferred_element_type=jnp.float32)
    sigmoid_pre = jax.nn.sigmoid(preact)
    hidden = (preact * sigmoid_pre).astype(jnp.bfloat16)
    silu_slope = sigmoid_pre * (1.0 + preact * (1.0 - sigmoid_pre))
    grad_pre = (cotangent.astype(jnp.float32) * silu_slope).astype(jnp.bfloat16)
    grad_scale = 1.0 / math.sqrt(NODES)
    grad_self = jnp.dot(features.T, grad_pre, preferred_element_type=jnp.float32) * grad_scale
    grad_neigh = jnp.dot(aggregate.T, grad_pre, preferred_element_type=jnp.float32) * grad_scale
    back_proj = (jnp.dot(grad_pre, w_neigh.T, preferred_element_type=jnp.float32) / root_deg).astype(jnp.bfloat16)
    back_panels = back_proj.reshape(PARTITIONS, BLOCKS_DEV, TILE, D)
    own_term = jnp.dot(grad_pre, w_self.T, preferred_element_type=jnp.float32)

    def backward_part(col_part):
        sources = (col_part - offset_ids + half_span) % PARTITIONS
        tiles = tile_vals[sources, offset_ids].astype(jnp.float32) * tile_live[sources, offset_ids].astype(jnp.float32)[:, :, None, None]
        row_blocks = tile_coords[sources, offset_ids, :, 0]
        col_blocks = tile_coords[sources, offset_ids, :, 1]
        picked = back_panels[sources[:, None], row_blocks]
        products = jnp.einsum('qkrc,qkrd->qkcd', tiles, picked.astype(jnp.float32))
        onehot = (col_blocks[None] == block_ids[:, None, None]).astype(jnp.float32)
        placed = jnp.einsum('jqk,qkcd->jcd', onehot, products, precision=lax.Precision.HIGHEST)
        return placed.reshape(ROWS_DEV, D)
    neighbour = lax.map(backward_part, jnp.arange(PARTITIONS, dtype=jnp.int32)).reshape(NODES, D)
    grad_features = (own_term + neighbour).astype(jnp.bfloat16)
    return (hidden, grad_features, grad_self, grad_neigh)
```

```python
import math

import jax
import jax.numpy as jnp
from jax import lax
from jax.experimental import pallas as pl
from jax.experimental.pallas import tpu as pltpu
from jax.sharding import PartitionSpec as P

BOTH = ("blk", "rep")
BF16 = jnp.bfloat16
F32 = jnp.float32
VMEM = pl.BlockSpec(memory_space=pltpu.VMEM)
SMEM = pl.BlockSpec(memory_space=pltpu.SMEM)


def exchange(value, target):
    part_total, rep_count = lax.axis_size("blk"), lax.axis_size("rep")
    pairs = []
    for part in range(part_total):
        for rep in range(rep_count):
            to_part, to_rep = target(part, rep)
            pairs.append((part * rep_count + rep, (to_part % part_total) * rep_count + to_rep))
    return lax.ppermute(value, BOTH, pairs)


def dot(lhs, rhs, contract):
    return lax.dot_general(lhs, rhs, (contract, ((), ())), preferred_element_type=F32)


def place_tiles(slot, out_axis, coords, live, tiles, source, total):
    tile_count, size = tiles.shape[-3], tiles.shape[-1]
    spare = total.shape[0] // size - 1
    for k in range(tile_count):
        to = jnp.where(live[0, slot, k] != 0, coords[0, slot, k, out_axis], spare)
        take = coords[0, slot, k, 1 - out_axis]
        tile = tiles[0, slot, k]
        block = source[pl.ds(pl.multiple_of(take * size, size), size), :]
        rows = pl.ds(pl.multiple_of(to * size, size), size)
        total[rows, :] += dot(tile, block, ((1 - out_axis,), (0,)))


def forward_first(coords, live, tiles, low, high, out, source, total):
    half = low.shape[0]
    source[:half, :] = low[...]
    source[half:, :] = high[...]
    total[...] = jnp.zeros_like(total)
    place_tiles(0, 0, coords, live, tiles, source, total)
    out[...] = total[: out.shape[0], :]


def forward_second(coords, live, tiles, low, high, before, keep, send, source, total):
    half = low.shape[0]
    rows = before.shape[0]
    source[:half, :] = low[...]
    source[half:, :] = high[...]
    total[:rows, :] = before[...]
    total[rows:, :] = jnp.zeros((total.shape[0] - rows, total.shape[1]), F32)
    place_tiles(1, 0, coords, live, tiles, source, total)
    core = lax.rem(lax.axis_index("rep"), 2)
    share = rows // 4
    for h in range(2):
        mine = pl.ds(pl.multiple_of((2 * h + core) * share, share), share)
        other = pl.ds(pl.multiple_of((2 * h + 1 - core) * share, share), share)
        keep[h] = total[mine, :]
        send[h] = total[other, :].astype(BF16)


def middle(chip_sum, far_sum, inv_root, self_term, cotangent, w_neigh, agg, hidden, grad_pre, back):
    summed = chip_sum[...] + far_sum[...].astype(F32)
    inv = inv_root[...]
    aggregate = (summed * inv).astype(BF16)
    agg[...] = aggregate
    preact = self_term[...] + dot(aggregate, w_neigh[...], ((1,), (0,)))
    sig = jax.nn.sigmoid(preact)
    hidden[...] = (preact * sig).astype(BF16)
    slope = sig * (1.0 + preact * (1.0 - sig))
    grad = (cotangent[...].astype(F32) * slope).astype(BF16)
    grad_pre[...] = grad
    back[...] = (dot(grad, w_neigh[...], ((1,), (1,))) * inv).astype(BF16)


def backward(coords, live, tiles, own, other, same0, cross0, same1, cross1, source, total):
    rep = lax.axis_index("rep")
    core, plane = lax.rem(rep, 2), lax.div(rep, 2)
    share = own.shape[1]
    for h in range(2):
        source[pl.ds(pl.multiple_of((2 * h + core) * share, share), share), :] = own[h]
        source[pl.ds(pl.multiple_of((2 * h + 1 - core) * share, share), share), :] = other[h]
    half = 2 * share
    for slot, (same, cross) in enumerate(((same0, cross0), (same1, cross1))):
        total[...] = jnp.zeros_like(total)
        place_tiles(slot, 1, coords, live, tiles, source, total)
        same[...] = total[pl.ds(pl.multiple_of(plane * half, half), half), :].astype(BF16)
        cross[...] = total[pl.ds(pl.multiple_of((1 - plane) * half, half), half), :].astype(BF16)


def on_device(tile_vals, tile_coords, tile_live, features, degree, w_self, w_neigh, cotangent):
    part_total = lax.axis_size("blk")
    rep_count = lax.axis_size("rep")
    rep = lax.axis_index("rep")
    core, plane = rep % 2, rep // 2
    slots = tile_vals.shape[1]
    half_span = slots * rep_count // 2
    tile_size = tile_vals.shape[3]
    rows, dim = features.shape
    half, share = rows // 2, rows // rep_count

    def shift(r, j):
        return slots * r + j - half_span

    def flip_core(value):
        return exchange(value, lambda b, r: (b, r ^ 1))

    def flip_plane(value):
        return exchange(value, lambda b, r: (b, r ^ 2))

    low, high = features[:half], features[half:]
    panels = []
    for j in range(slots):
        panels.append(
            (
                exchange(low, lambda b, r: (b - shift(r, j), r)),
                exchange(high, lambda b, r: (b - shift(r ^ 2, j), r ^ 2)),
            )
        )

    cot_far = flip_plane(cotangent)
    deg = degree.astype(F32)
    quarters = features.reshape(2, 2, share, dim)
    own_rows = lax.dynamic_index_in_dim(quarters, core, 1, keepdims=False)
    own_rows = own_rows.reshape(half, dim)
    cot = jnp.where(plane == 0, jnp.stack([cotangent, cot_far]), jnp.stack([cot_far, cotangent])).reshape(half, dim)
    deg_far = flip_plane(degree)
    deg = jnp.where(plane == 0, jnp.stack([degree, deg_far]), jnp.stack([deg_far, degree])).astype(F32)
    inv_root = jnp.broadcast_to((1.0 / jnp.sqrt(deg)).reshape(half, 1), (half, dim))
    self_term = jnp.dot(own_rows, w_self, preferred_element_type=F32)

    scratch = [pltpu.VMEM((rows, dim), BF16), pltpu.VMEM((rows + tile_size, dim), F32)]
    spec_in = [SMEM, SMEM, VMEM]
    first = pl.pallas_call(
        forward_first,
        out_shape=jax.ShapeDtypeStruct((rows, dim), F32),
        in_specs=spec_in + [VMEM] * 2,
        out_specs=VMEM,
        scratch_shapes=scratch,
        name="forward_first",
    )(tile_coords, tile_live, tile_vals, *panels[0])
    keep, send = pl.pallas_call(
        forward_second,
        out_shape=[jax.ShapeDtypeStruct((2, share, dim), F32), jax.ShapeDtypeStruct((2, share, dim), BF16)],
        in_specs=spec_in + [VMEM] * 3,
        out_specs=[VMEM] * 2,
        scratch_shapes=scratch,
        name="forward_second",
    )(tile_coords, tile_live, tile_vals, *panels[1], first)

    chip_sum = (keep + flip_core(send).astype(F32)).reshape(half, dim)
    far_sum = flip_plane(chip_sum.astype(BF16))
    wide = jax.ShapeDtypeStruct((half, dim), BF16)
    agg, hidden_both, grad_pre, back = pl.pallas_call(
        middle,
        out_shape=[wide] * 4,
        in_specs=[VMEM] * 6,
        out_specs=[VMEM] * 4,
        name="middle",
    )(chip_sum, far_sum, inv_root, self_term, cot, w_neigh)

    back = back.reshape(2, share, dim)
    other_back = flip_core(back)
    piece = jax.ShapeDtypeStruct((half, dim), BF16)
    sends = pl.pallas_call(
        backward,
        out_shape=[piece] * 4,
        in_specs=spec_in + [VMEM] * 2,
        out_specs=[VMEM] * 4,
        scratch_shapes=scratch,
        name="backward",
    )(tile_coords, tile_live, tile_vals, back, other_back)

    arrived = []
    for j in range(slots):
        arrived.append(exchange(sends[2 * j], lambda b, r: (b + shift(r, j), r)))
        arrived.append(exchange(sends[2 * j + 1], lambda b, r: (b + shift(r, j), r ^ 2)))

    left = jnp.where(plane == 0, own_rows, agg)
    local = jnp.einsum("nd,ne->de", left, grad_pre, preferred_element_type=F32).reshape(2, dim // 2, dim)
    mine = lax.dynamic_index_in_dim(local, core, 0, keepdims=False)
    theirs = lax.dynamic_index_in_dim(local, 1 - core, 0, keepdims=False)
    grad = mine + flip_core(theirs.astype(BF16)).astype(F32)
    bit = 1
    while bit < part_total:
        rounded = grad.astype(BF16)
        grad = rounded.astype(F32) + exchange(rounded, lambda b, r: (b ^ bit, r)).astype(F32)
        bit *= 2
    rounded = grad.astype(BF16)
    far = flip_plane(rounded)
    by_plane = jnp.where(plane == 0, jnp.stack([rounded, far]), jnp.stack([far, rounded]))
    near = flip_core(by_plane)
    by_core = jnp.where(core == 0, jnp.stack([by_plane, near], 1), jnp.stack([near, by_plane], 1))
    grad_scale = 1.0 / math.sqrt(rows * part_total)
    totals = by_core.reshape(2, dim, dim).astype(F32) * grad_scale

    grad_pre_own = lax.dynamic_index_in_dim(grad_pre.reshape(2, share, dim), plane, 0, keepdims=False)
    own_term = jnp.einsum("ne,de->nd", grad_pre_own, w_self, preferred_element_type=F32)
    neighbour = sum(a.astype(F32) for a in arrived).reshape(2, share, dim)
    near = flip_core(lax.dynamic_index_in_dim(neighbour, 1 - core, 0, keepdims=False).astype(BF16))
    neighbour = lax.dynamic_index_in_dim(neighbour, core, 0, keepdims=False) + near.astype(F32)
    grad_features = (own_term + neighbour).astype(BF16)
    hidden = lax.dynamic_index_in_dim(hidden_both.reshape(2, share, dim), plane, 0, keepdims=False)
    return (hidden, grad_features, totals[0], totals[1])


def solution(mesh):
    return jax.shard_map(
        on_device,
        mesh=mesh,
        in_specs=(
            P("blk", "rep", None, None, None),
            P("blk", "rep", None, None),
            P("blk", "rep", None),
            P("blk", None),
            P(("blk", "rep")),
            P(),
            P(),
            P(("blk", "rep"), None),
        ),
        out_specs=(P(("blk", "rep"), None), P(("blk", "rep"), None), P(), P()),
        check_vma=False,
    )
```

```python
import math

import jax
import jax.numpy as jnp
from jax import lax
from jax.experimental import pallas as pl
from jax.experimental.pallas import tpu as pltpu
from jax.sharding import PartitionSpec as P

BOTH = ("blk", "rep")
BF16 = jnp.bfloat16
F32 = jnp.float32
VMEM = pl.BlockSpec(memory_space=pltpu.VMEM)
SMEM = pl.BlockSpec(memory_space=pltpu.SMEM)


def exchange(value, target):
    part_total, rep_count = lax.axis_size("blk"), lax.axis_size("rep")
    pairs = []
    for part in range(part_total):
        for rep in range(rep_count):
            to_part, to_rep = target(part, rep)
            pairs.append((part * rep_count + rep, (to_part % part_total) * rep_count + to_rep))
    return lax.ppermute(value, BOTH, pairs)


def dot(lhs, rhs, contract):
    return lax.dot_general(lhs, rhs, (contract, ((), ())), preferred_element_type=F32)


def place_tiles(slot, out_axis, meta, tiles, source, total):
    size = tiles.shape[-1]
    tile_count = tiles.shape[-3]
    for k in range(tile_count):
        to = meta[out_axis, slot * tile_count + k]
        take = meta[3 - out_axis, slot * tile_count + k]
        block = source[pl.ds(pl.multiple_of(take * size, size), size), :]
        rows = pl.ds(pl.multiple_of(to * size, size), size)
        total[rows, :] += dot(tiles[0, slot, k], block, ((1 - out_axis,), (0,)))


def forward_first(meta, tiles, local, arrived, out, source, total):
    is_local = lax.axis_index("rep") == local_rep(tiles.shape[1])

    @pl.when(is_local)
    def _():
        source[...] = local[...]

    @pl.when(jnp.logical_not(is_local))
    def _():
        source[...] = arrived[...]

    total[...] = jnp.zeros_like(total)
    place_tiles(0, 0, meta, tiles, source, total)
    out[...] = total[: out.shape[0], :]


def forward_second(meta, tiles, arrived, before, keep, send, total):
    rows = before.shape[0]
    total[:rows, :] = before[...]
    total[rows:, :] = jnp.zeros((total.shape[0] - rows, total.shape[1]), F32)
    place_tiles(1, 0, meta, tiles, arrived, total)
    core = lax.rem(lax.axis_index("rep"), 2)
    share = rows // 4
    for h in range(2):
        mine = pl.ds(pl.multiple_of((2 * h + core) * share, share), share)
        other = pl.ds(pl.multiple_of((2 * h + 1 - core) * share, share), share)
        keep[h * share : (h + 1) * share, :] = total[mine, :]
        send[h * share : (h + 1) * share, :] = total[other, :].astype(BF16)


def prepare(
    coords, live, tiles, features, cot_own, deg_own, w_self, cot_far, deg_far,
    meta, kept_tiles, own_rows, self_term, cot, inv_root, deg_near, weights, sems,
):
    rep = lax.axis_index("rep")
    core, plane = lax.rem(rep, 2), lax.div(rep, 2)
    share = cot_own.shape[0]
    near = pl.ds(pl.multiple_of(plane * share, share), share)
    away = pl.ds(pl.multiple_of((1 - plane) * share, share), share)
    pairs = [(tiles, kept_tiles), (cot_own, cot.at[near]), (deg_own, deg_near), (w_self, weights)]
    for h in range(2):
        rows = features.at[pl.ds(pl.multiple_of((2 * h + core) * share, share), share)]
        pairs.append((rows, own_rows.at[h * share : (h + 1) * share]))
    copies = [pltpu.make_async_copy(*pair, sems.at[i]) for i, pair in enumerate(pairs)]
    for copy in copies:
        copy.start()
    slots, tile_count = live.shape[1:]
    spare = features.shape[0] // kept_tiles.shape[-1]
    for slot in range(slots):
        for k in range(tile_count):
            at = slot * tile_count + k
            present = live[0, slot, k] != 0
            row, column = coords[0, slot, k, 0], coords[0, slot, k, 1]
            meta[0, at] = jnp.where(present, row, spare)
            meta[1, at] = jnp.where(present, column, spare)
            meta[2, at] = row
            meta[3, at] = column
    for copy in copies:
        copy.wait()
    cot[away, :] = cot_far[...]
    width = inv_root.shape[1]
    for where, deg in ((near, deg_near), (away, deg_far)):
        inv_root[where, :] = jnp.transpose(jnp.broadcast_to(1.0 / jnp.sqrt(deg[...].astype(F32)), (width, share)))
    self_term[...] = dot(own_rows[...], weights[...], ((1,), (0,)))


def middle(chip_sum, far_sum, inv_root, self_term, cot, own_rows, w_self, w_neigh, hidden, own_term, message, kept_grad, grads):
    rep = lax.axis_index("rep")
    core, plane = lax.rem(rep, 2), lax.div(rep, 2)
    half, share = chip_sum.shape[0], hidden.shape[0]
    inv = inv_root[...]
    aggregate = ((chip_sum[...] + far_sum[...].astype(F32)) * inv).astype(BF16)
    preact = self_term[...] + dot(aggregate, w_neigh[...], ((1,), (0,)))
    sig = jax.nn.sigmoid(preact)
    slope = sig * (1.0 + preact * (1.0 - sig))
    grad = (cot[...].astype(F32) * slope).astype(BF16)
    message[:half, :] = (dot(grad, w_neigh[...], ((1,), (1,))) * inv).astype(BF16)
    left = jnp.where(plane == 0, own_rows[...].astype(F32), aggregate.astype(F32)).astype(BF16)
    grads[...] = dot(left, grad, ((0,), (0,)))
    rows = kept_grad.shape[0]
    kept_grad[...] = grads[pl.ds(pl.multiple_of(core * rows, rows), rows), :]
    message[half:, :] = grads[pl.ds(pl.multiple_of((1 - core) * rows, rows), rows), :].astype(BF16)
    value = (preact * sig).astype(BF16)
    term = dot(grad, w_self[...], ((1,), (1,)))

    @pl.when(plane == 0)
    def _():
        hidden[...] = value[:share]
        own_term[...] = term[:share]

    @pl.when(plane != 0)
    def _():
        hidden[...] = value[share:]
        own_term[...] = term[share:]


def backward(meta, tiles, own, other, far_cross, far_same, near_cross, near_same, source, total):
    rep = lax.axis_index("rep")
    core, plane = lax.rem(rep, 2), lax.div(rep, 2)
    share = source.shape[0] // 4
    for h in range(2):
        part = slice(h * share, (h + 1) * share)
        source[pl.ds(pl.multiple_of((2 * h + core) * share, share), share), :] = own[part, :]
        source[pl.ds(pl.multiple_of((2 * h + 1 - core) * share, share), share), :] = other[part, :]
    half = 2 * share
    for slot, cross, same in ((plane, far_cross, far_same), (1 - plane, near_cross, near_same)):
        total[...] = jnp.zeros_like(total)
        place_tiles(slot, 1, meta, tiles, source, total)
        cross[...] = total[pl.ds(pl.multiple_of((1 - plane) * half, half), half), :].astype(BF16)
        same[...] = total[pl.ds(pl.multiple_of(plane * half, half), half), :].astype(BF16)


def local_rep(slots):
    return (slots * lax.axis_size("rep") // 2) // slots


def kernel_call(kernel, name, outs, args, scratch=(), in_specs=None, out_specs=None):
    return pl.pallas_call(
        kernel,
        out_shape=[jax.ShapeDtypeStruct(*out) for out in outs],
        in_specs=in_specs or [VMEM] * len(args),
        out_specs=out_specs or [VMEM] * len(outs),
        scratch_shapes=scratch,
        compiler_params=pltpu.CompilerParams(vmem_limit_bytes=8 * 2**20),
        name=name,
    )(*args)


def on_device(tile_vals, tile_coords, tile_live, features, degree, w_self, w_neigh, cotangent):
    part_total = lax.axis_size("blk")
    rep_count = lax.axis_size("rep")
    rep = lax.axis_index("rep")
    core, plane = rep % 2, rep // 2
    slots, tile_count, tile_size = tile_vals.shape[1:4]
    half_span = slots * rep_count // 2
    rows, dim = features.shape
    half, share = rows // 2, rows // rep_count

    def shift(r, j):
        return slots * r + j - half_span

    def flip_core(value):
        return exchange(value, lambda b, r: (b, r ^ 1))

    def flip_plane(value):
        return exchange(value, lambda b, r: (b, r ^ 2))

    home = local_rep(slots)
    pairs = []
    for part in range(part_total):
        for r in range(rep_count):
            if r == home:
                continue
            giver = home if r == home - 1 else r
            pairs.append((((part + shift(r, 0)) % part_total) * rep_count + giver, part * rep_count + r))
    panel_first = lax.ppermute(features, BOTH, pairs)
    panel_second = exchange(features, lambda b, r: (b - shift(r, 1), r))

    degree = degree.reshape(1, share)
    wide = (half, dim)
    cot_far, deg_far = flip_plane(cotangent), flip_plane(degree)
    raw = [tile_coords, tile_live, tile_vals, features, cotangent, degree, w_self]
    raw = [pltpu.with_memory_space_constraint(a, pltpu.HBM) for a in raw]
    meta, tiles, own_rows, self_term, cot, inv_root = kernel_call(
        prepare,
        "prepare",
        [((4, slots * tile_count), jnp.int32), (tile_vals.shape, BF16), (wide, BF16), (wide, F32), (wide, BF16), (wide, F32)],
        raw + [cot_far, deg_far],
        [pltpu.VMEM((1, share), jnp.int32), pltpu.VMEM(w_self.shape, BF16), pltpu.SemaphoreType.DMA((6,))],
        [SMEM] * 2 + [pl.BlockSpec(memory_space=pltpu.HBM)] * 5 + [VMEM] * 2,
        [SMEM] + [VMEM] * 5,
    )

    source, total = pltpu.VMEM((rows, dim), BF16), pltpu.VMEM((rows + tile_size, dim), F32)
    first = kernel_call(
        forward_first, "forward_first", [((rows, dim), F32)], [meta, tiles, features, panel_first], [source, total],
        [SMEM] + [VMEM] * 3,
    )[0]
    keep, send = kernel_call(
        forward_second, "forward_second", [(wide, F32), (wide, BF16)], [meta, tiles, panel_second, first], [total],
        [SMEM] + [VMEM] * 3,
    )
    chip_sum = keep + flip_core(send).astype(F32)
    far_sum = flip_plane(chip_sum.astype(BF16))

    grad_rows = dim // 2
    hidden, own_term, message, kept_grad = kernel_call(
        middle,
        "middle",
        [((share, dim), BF16), ((share, dim), F32), ((half + grad_rows, dim), BF16), ((grad_rows, dim), F32)],
        [chip_sum, far_sum, inv_root, self_term, cot, own_rows, w_self, w_neigh],
        [pltpu.VMEM((dim, dim), F32)],
    )
    other = flip_core(message)
    sends = kernel_call(
        backward, "backward", [(wide, BF16)] * 4, [meta, tiles, message, other], [source, total], [SMEM] + [VMEM] * 3
    )

    def far(r):
        return shift(r, r // 2)

    def near(r):
        return shift(r, 1 - r // 2)

    arrived = [
        exchange(sends[0], lambda b, r: (b + far(r), r ^ 2)),
        exchange(sends[1], lambda b, r: (b + far(r), r)),
        exchange(sends[2], lambda b, r: (b + near(r), r ^ 2)),
        exchange(sends[3], lambda b, r: (b + near(r), r)),
    ]

    rounded = (kept_grad + other[half:].astype(F32)).astype(BF16)

    def others(value, bit):
        return exchange(value, lambda b, r: (b ^ bit, r)).astype(F32)

    grad = rounded.astype(F32)
    bits = [1 << i for i in range(part_total.bit_length() - 2, -1, -1)]
    for i, bit in enumerate(bits):
        rounded = grad.astype(BF16)
        come = others(rounded, bit)
        if i == 0:
            come, _ = lax.optimization_barrier((come, sends[0]))
        if i == 1:
            come, _ = lax.optimization_barrier((come, arrived[0]))
        grad = rounded.astype(F32) + come
    rounded = grad.astype(BF16)
    twin = flip_plane(rounded)
    by_plane = jnp.where(plane == 0, jnp.stack([rounded, twin]), jnp.stack([twin, rounded]))
    twin = flip_core(by_plane)
    by_core = jnp.where(core == 0, jnp.stack([by_plane, twin], 1), jnp.stack([twin, by_plane], 1))
    grad_scale = 1.0 / math.sqrt(rows * part_total)
    totals = by_core.reshape(2, dim, dim).astype(F32) * grad_scale

    neighbour = sum(a.astype(F32) for a in arrived).reshape(2, share, dim)
    twin = flip_core(lax.dynamic_index_in_dim(neighbour, 1 - core, 0, keepdims=False).astype(BF16))
    neighbour = lax.dynamic_index_in_dim(neighbour, core, 0, keepdims=False) + twin.astype(F32)
    grad_features = (own_term + neighbour).astype(BF16)
    return (hidden, grad_features, totals[0], totals[1])


def solution(mesh):
    return jax.shard_map(
        on_device,
        mesh=mesh,
        in_specs=(
            P("blk", "rep", None, None, None),
            P("blk", "rep", None, None),
            P("blk", "rep", None),
            P("blk", None),
            P(("blk", "rep")),
            P(),
            P(),
            P(("blk", "rep"), None),
        ),
        out_specs=(P(("blk", "rep"), None), P(("blk", "rep"), None), P(), P()),
        check_vma=False,
    )
```

```python
import functools
import math

import jax
import jax.numpy as jnp
from jax import lax
from jax.experimental import pallas as pl
from jax.experimental.pallas import tpu as pltpu
from jax.sharding import PartitionSpec as P

BOTH = ("blk", "rep")
PIECES = 1
BF16 = jnp.bfloat16
F32 = jnp.float32
VMEM = pl.BlockSpec(memory_space=pltpu.VMEM)
SMEM = pl.BlockSpec(memory_space=pltpu.SMEM)


def exchange(value, target):
    part_total, rep_count = lax.axis_size("blk"), lax.axis_size("rep")
    pairs = []
    for part in range(part_total):
        for rep in range(rep_count):
            to_part, to_rep = target(part, rep)
            pairs.append((part * rep_count + rep, (to_part % part_total) * rep_count + to_rep))
    return lax.ppermute(value, BOTH, pairs)


def dot(lhs, rhs, contract):
    return lax.dot_general(lhs, rhs, (contract, ((), ())), preferred_element_type=F32)


def place_tiles(slot, out_axis, meta, tiles, source, total):
    size = tiles.shape[-1]
    tile_count = tiles.shape[-3]
    for k in range(tile_count):
        to = meta[out_axis, slot * tile_count + k]
        take = meta[3 - out_axis, slot * tile_count + k]
        block = source[pl.ds(pl.multiple_of(take * size, size), size), :]
        rows = pl.ds(pl.multiple_of(to * size, size), size)
        total[rows, :] += dot(tiles[slot, k], block, ((1 - out_axis,), (0,)))


def forward_first(meta, tiles, arrived, out, total):
    total[...] = jnp.zeros_like(total)
    place_tiles(0, 0, meta, tiles, arrived, total)
    out[...] = total[: out.shape[0], :]


def forward_second(swap, meta, tiles, arrived, panel, before, keep, send, source, total):
    rows = before.shape[0]
    total[:rows, :] = before[...]
    total[rows:, :] = jnp.zeros((total.shape[0] - rows, total.shape[1]), F32)
    is_local = near_is_local(swap, lax.axis_index("blk"), lax.axis_index("rep"))

    @pl.when(is_local)
    def _():
        source[...] = panel[...]

    @pl.when(jnp.logical_not(is_local))
    def _():
        source[...] = arrived[...]

    place_tiles(1, 0, meta, tiles, source, total)
    core = lax.rem(lax.axis_index("rep"), 2)
    share = rows // 4
    for h in range(2):
        mine = pl.ds(pl.multiple_of((2 * h + core) * share, share), share)
        other = pl.ds(pl.multiple_of((2 * h + 1 - core) * share, share), share)
        keep[h * share : (h + 1) * share, :] = total[mine, :]
        send[h * share : (h + 1) * share, :] = total[other, :].astype(BF16)


def prepare(
    swap, coords, live, far_note, tiles, features, cot_own, deg_own, w_self, cot_far, deg_far, *rest,
):
    moved = rest[:-9]
    meta, kept_tiles, panel, self_term, cot, inv_root, deg_near, weights, sems = rest[-9:]
    rep = lax.axis_index("rep")
    core, plane = lax.rem(rep, 2), lax.div(rep, 2)
    share = cot_own.shape[0]
    near = pl.ds(pl.multiple_of(plane * share, share), share)
    away = pl.ds(pl.multiple_of((1 - plane) * share, share), share)
    pairs = [(cot_own, cot.at[near]), (deg_own, deg_near), (w_self, weights), (features, panel)]
    copies = [pltpu.make_async_copy(*pair, sems.at[i]) for i, pair in enumerate(pairs)]
    for copy in copies:
        copy.start()

    swaps = swaps_slot(swap, lax.axis_index("blk"), rep)
    far_moved = jnp.logical_and(swaps, plane == 1)
    near_moved = jnp.logical_and(swaps, plane == 0)
    slot_of = (plane, jnp.where(far_moved, 1, 1 - plane))
    tile_copies = []
    for order, is_moved in enumerate((far_moved, near_moved)):
        place = kept_tiles.at[order]
        here = pltpu.make_async_copy(tiles.at[0, slot_of[order]], place, sems.at[len(tile_copies) + 5])
        tile_copies.append((jnp.logical_not(is_moved), here))
        start = 0
        for piece in moved:
            part = place.at[start : start + piece.shape[0]]
            tile_copies.append((is_moved, pltpu.make_async_copy(piece, part, sems.at[len(tile_copies) + 5])))
            start += piece.shape[0]
    for is_needed, copy in tile_copies:
        pl.when(is_needed)(copy.start)

    tile_count = live.shape[2]
    spare = features.shape[0] // kept_tiles.shape[-1]
    for order, is_moved in enumerate((far_moved, near_moved)):
        slot = slot_of[order]
        for k in range(tile_count):
            at = order * tile_count + k
            row = jnp.where(is_moved, far_note[share + 2 * k], coords[0, slot, k, 0])
            column = jnp.where(is_moved, far_note[share + 2 * k + 1], coords[0, slot, k, 1])
            present = jnp.where(is_moved, far_note[share + 2 * tile_count + k], live[0, slot, k]) != 0
            meta[0, at] = jnp.where(present, row, spare)
            meta[1, at] = jnp.where(present, column, spare)
            meta[2, at] = row
            meta[3, at] = column
    for copy in copies:
        copy.wait()
    cot[away, :] = cot_far[...]
    width = inv_root.shape[1]
    for where, deg in ((near, deg_near[...]), (away, deg_far[:1, :])):
        inv_root[where, :] = jnp.transpose(jnp.broadcast_to(1.0 / jnp.sqrt(deg.astype(F32)), (width, share)))
    for h in range(2):
        rows = panel[pl.ds(pl.multiple_of((2 * h + core) * share, share), share), :]
        self_term[h * share : (h + 1) * share, :] = dot(rows, weights[...], ((1,), (0,)))
    for is_needed, copy in tile_copies:
        pl.when(is_needed)(copy.wait)


def middle(chip_sum, far_sum, inv_root, self_term, cot, panel, w_self, w_neigh, hidden, own_term, message, kept_grad, grads):
    rep = lax.axis_index("rep")
    core, plane = lax.rem(rep, 2), lax.div(rep, 2)
    half, share = chip_sum.shape[0], hidden.shape[0]
    inv = inv_root[...]
    aggregate = ((chip_sum[...] + far_sum[...].astype(F32)) * inv).astype(BF16)
    preact = self_term[...] + dot(aggregate, w_neigh[...], ((1,), (0,)))
    sig = jax.nn.sigmoid(preact)
    slope = sig * (1.0 + preact * (1.0 - sig))
    grad = (cot[...].astype(F32) * slope).astype(BF16)
    message[:half, :] = (dot(grad, w_neigh[...], ((1,), (1,))) * inv).astype(BF16)

    @pl.when(plane == 0)
    def _():
        own = [panel[pl.ds(pl.multiple_of((2 * h + core) * share, share), share), :] for h in range(2)]
        grads[...] = dot(own[0], grad[:share], ((0,), (0,))) + dot(own[1], grad[share:], ((0,), (0,)))

    @pl.when(plane != 0)
    def _():
        grads[...] = dot(aggregate, grad, ((0,), (0,)))

    rows = kept_grad.shape[0]
    kept_grad[...] = grads[pl.ds(pl.multiple_of(core * rows, rows), rows), :]
    message[half:, :] = grads[pl.ds(pl.multiple_of((1 - core) * rows, rows), rows), :].astype(BF16)
    value = (preact * sig).astype(BF16)
    term = dot(grad, w_self[...], ((1,), (1,)))

    @pl.when(plane == 0)
    def _():
        hidden[...] = value[:share]
        own_term[...] = term[:share]

    @pl.when(plane != 0)
    def _():
        hidden[...] = value[share:]
        own_term[...] = term[share:]


def backward(swap, meta, tiles, own, other, far_cross, far_same, near_first, near_last, source, total):
    rep = lax.axis_index("rep")
    core, plane = lax.rem(rep, 2), lax.div(rep, 2)
    share = source.shape[0] // 4
    for h in range(2):
        part = slice(h * share, (h + 1) * share)
        source[pl.ds(pl.multiple_of((2 * h + core) * share, share), share), :] = own[part, :]
        source[pl.ds(pl.multiple_of((2 * h + 1 - core) * share, share), share), :] = other[part, :]
    half = 2 * share
    same_first = home_first(swap, lax.axis_index("blk"), rep)
    to_plane = jnp.where(same_first, plane, 1 - plane)
    for slot, outs in enumerate(((far_cross, far_same), (near_first, near_last))):
        total[...] = jnp.zeros_like(total)
        place_tiles(slot, 1, meta, tiles, source, total)
        first = 1 - plane if slot == 0 else to_plane
        for out, which in zip(outs, (first, 1 - first)):
            out[...] = total[pl.ds(pl.multiple_of(which * half, half), half), :].astype(BF16)


def swaps_slot(swap, part, rep):
    return (part % 2 == 0) & (rep % 2 == 0) & swap


def near_is_local(swap, part, rep):
    return rep == (2 * (part % 2) if swap else 2)


def home_first(swap, part, rep):
    return (rep == 2 * (part % 2)) & swap


def kernel_call(kernel, name, outs, args, scratch=(), in_specs=None, out_specs=None):
    return pl.pallas_call(
        kernel,
        out_shape=[jax.ShapeDtypeStruct(*out) for out in outs],
        in_specs=in_specs or [VMEM] * len(args),
        out_specs=out_specs or [VMEM] * len(outs),
        scratch_shapes=scratch,
        compiler_params=pltpu.CompilerParams(vmem_limit_bytes=8 * 2**20),
        name=name,
    )(*args)


def on_device(tile_vals, tile_coords, tile_live, features, degree, w_self, w_neigh, cotangent):
    part_total = lax.axis_size("blk")
    rep_count = lax.axis_size("rep")
    rep = lax.axis_index("rep")
    core, plane = rep % 2, rep // 2
    slots, tile_count, tile_size = tile_vals.shape[1:4]
    half_span = slots * rep_count // 2
    rows, dim = features.shape
    half, share = rows // 2, rows // rep_count

    swap = part_total == slots * rep_count

    def far(part, r):
        if swap and r == 2 and part % 2 == 0:
            return 1 - half_span
        return slots * r + r // 2 - half_span

    def near(part, r):
        if swap and r in (0, 2) and part % 2 == 0:
            return 0 if r == 0 else 1
        return slots * r + 1 - r // 2 - half_span

    def flip_core(value):
        return exchange(value, lambda b, r: (b, r ^ 1))

    def flip_plane(value):
        return exchange(value, lambda b, r: (b, r ^ 2))

    def fetch(shift):
        pairs = []
        for part in range(part_total):
            for r in range(rep_count):
                if shift(part, r):
                    pairs.append((((part + shift(part, r)) % part_total) * rep_count + r, part * rep_count + r))
        return lax.ppermute(features, BOTH, pairs)

    panel_far, panel_near = fetch(far), fetch(near)

    def note_of(slot):
        parts = [degree, tile_coords[0, slot].reshape(-1), tile_live[0, slot]]
        parts.append(jnp.zeros((2 * share - sum(p.size for p in parts),), jnp.int32))
        return jnp.concatenate(parts)

    far_note = flip_plane(jnp.where(plane == 0, note_of(1), note_of(0)))
    cot_far = flip_plane(cotangent)
    moved = []
    if swap:
        pairs = []
        for part in range(0, part_total, 2):
            pairs += [(part * rep_count, part * rep_count + 2), (part * rep_count + 2, part * rep_count)]
        cuts = [tile_count * i // PIECES for i in range(PIECES + 1)]
        for low, high in zip(cuts, cuts[1:]):
            piece = jnp.where(plane == 0, tile_vals[0, 1, low:high], tile_vals[0, 0, low:high])
            moved.append(lax.ppermute(piece, BOTH, pairs))
    wide = (half, dim)
    raw = [tile_vals, features, cotangent, degree.reshape(1, share), w_self]
    raw = [pltpu.with_memory_space_constraint(a, pltpu.HBM) for a in raw]
    meta, tiles, panel, self_term, cot, inv_root = kernel_call(
        functools.partial(prepare, swap),
        "prepare",
        [((4, slots * tile_count), jnp.int32), (tile_vals.shape[1:], BF16), ((rows, dim), BF16), (wide, F32), (wide, BF16), (wide, F32)],
        [tile_coords, tile_live, far_note] + raw + [cot_far, far_note.reshape(2, share)] + moved,
        [pltpu.VMEM((1, share), jnp.int32), pltpu.VMEM(w_self.shape, BF16), pltpu.SemaphoreType.DMA((7 + 2 * len(moved),))],
        [SMEM] * 3 + [pl.BlockSpec(memory_space=pltpu.HBM)] * 5 + [VMEM] * 2 + [pl.BlockSpec(memory_space=pl.ANY)] * len(moved),
        [SMEM] + [VMEM] * 5,
    )

    source, total = pltpu.VMEM((rows, dim), BF16), pltpu.VMEM((rows + tile_size, dim), F32)
    first = kernel_call(
        forward_first, "forward_first", [((rows, dim), F32)], [meta, tiles, panel_far], [total], [SMEM] + [VMEM] * 2
    )[0]
    keep, send = kernel_call(
        functools.partial(forward_second, swap), "forward_second", [(wide, F32), (wide, BF16)],
        [meta, tiles, panel_near, panel, first], [source, total], [SMEM] + [VMEM] * 4,
    )
    chip_sum = keep + flip_core(send).astype(F32)
    far_sum = flip_plane(chip_sum.astype(BF16))

    grad_rows = dim // 2
    hidden, own_term, message, kept_grad = kernel_call(
        middle,
        "middle",
        [((share, dim), BF16), ((share, dim), F32), ((half + grad_rows, dim), BF16), ((grad_rows, dim), F32)],
        [chip_sum, far_sum, inv_root, self_term, cot, panel, w_self, w_neigh],
        [pltpu.VMEM((dim, dim), F32)],
    )
    other = flip_core(message)
    sends = kernel_call(
        functools.partial(backward, swap), "backward", [(wide, BF16)] * 4, [meta, tiles, message, other], [source, total], [SMEM] + [VMEM] * 3
    )

    def others(value, bit, rep_bit=0):
        return exchange(value, lambda b, r: (b ^ bit, r ^ rep_bit))

    def added(one, two):
        return (one.astype(F32) + two.astype(F32)).astype(BF16)

    def tied(value, *after):
        return lax.optimization_barrier((value,) + after)[0]

    sends = list(sends)
    rounded = (kept_grad + other[half:].astype(F32)).astype(BF16)
    top = part_total.bit_length() - 2
    def near_first(part, r, flip):
        return (part + near(part, r), r if bool(home_first(swap, part, r)) != flip else r ^ 2)

    arrived = [
        exchange(sends[0], lambda b, r: (b + far(b, r), r ^ 2)),
        exchange(sends[1], lambda b, r: (b + far(b, r), r)),
        exchange(sends[2], lambda b, r: near_first(b, r, False)),
        exchange(sends[3], lambda b, r: near_first(b, r, True)),
    ]

    rounded = added(rounded, tied(others(rounded, 1 << top), sends[0]))
    rounded = added(rounded, tied(others(rounded, 2), arrived[0]))
    rounded = added(rounded, tied(others(rounded, 1), arrived[1]))
    twin = flip_plane(rounded)
    by_plane = jnp.where(plane == 0, jnp.stack([rounded, twin]), jnp.stack([twin, rounded]))
    twin = flip_core(by_plane)
    by_core = jnp.where(core == 0, jnp.stack([by_plane, twin], 1), jnp.stack([twin, by_plane], 1))
    grad_scale = 1.0 / math.sqrt(rows * part_total)
    totals = by_core.reshape(2, dim, dim).astype(F32) * grad_scale

    neighbour = sum(a.astype(F32) for a in arrived).reshape(2, share, dim)
    twin = flip_core(lax.dynamic_index_in_dim(neighbour, 1 - core, 0, keepdims=False).astype(BF16))
    neighbour = lax.dynamic_index_in_dim(neighbour, core, 0, keepdims=False) + twin.astype(F32)
    grad_features = (own_term + neighbour).astype(BF16)
    return (hidden, grad_features, totals[0], totals[1])


def solution(mesh):
    return jax.shard_map(
        on_device,
        mesh=mesh,
        in_specs=(
            P("blk", "rep", None, None, None),
            P("blk", "rep", None, None),
            P("blk", "rep", None),
            P("blk", None),
            P(("blk", "rep")),
            P(),
            P(),
            P(("blk", "rep"), None),
        ),
        out_specs=(P(("blk", "rep"), None), P(("blk", "rep"), None), P(), P()),
        check_vma=False,
    )
```

```python
import functools
import math

import jax
import jax.numpy as jnp
from jax import lax
from jax.experimental import pallas as pl
from jax.experimental.pallas import tpu as pltpu
from jax.sharding import PartitionSpec as P

BOTH = ("blk", "rep")
BF16 = jnp.bfloat16
F32 = jnp.float32
VMEM = pl.BlockSpec(memory_space=pltpu.VMEM)
SMEM = pl.BlockSpec(memory_space=pltpu.SMEM)


def exchange(value, target):
    part_total, rep_count = lax.axis_size("blk"), lax.axis_size("rep")
    pairs = []
    for part in range(part_total):
        for rep in range(rep_count):
            to_part, to_rep = target(part, rep)
            pairs.append((part * rep_count + rep, (to_part % part_total) * rep_count + to_rep))
    return lax.ppermute(value, BOTH, pairs)


def dot(lhs, rhs, contract):
    return lax.dot_general(lhs, rhs, (contract, ((), ())), preferred_element_type=F32)


def slot_of(swap, order, rep, part):
    plane = lax.div(rep, 2)
    swaps = swaps_slot(swap, part, rep)
    moved = jnp.logical_and(swaps, plane == 1 - order)
    if order == 0:
        return moved, plane
    return moved, jnp.where(jnp.logical_and(swaps, plane == 1), 1, 1 - plane)


def place_tiles(swap, order, out_axis, coords, live, note, tiles, source, total):
    size, tile_count = tiles.shape[-1], tiles.shape[-3]
    spare = total.shape[0] // size - 1
    moved, slot = slot_of(swap, order, lax.axis_index("rep"), lax.axis_index("blk"))
    at = note.shape[0] // 2
    for k in range(tile_count):
        places = [jnp.where(moved, note[at + 2 * k + axis], coords[0, slot, axis, k]) for axis in range(2)]
        present = jnp.where(moved, note[at + 2 * tile_count + k], live[0, slot, k]) != 0
        take, to = places[1 - out_axis], jnp.where(present, places[out_axis], spare)
        block = source[pl.ds(pl.multiple_of(take * size, size), size), :]
        rows = pl.ds(pl.multiple_of(to * size, size), size)
        total[rows, :] += dot(tiles[order, k], block, ((1 - out_axis,), (0,)))


def forward(swap, coords, live, note, tiles, far, near, panel, keep, send, source, total):
    rows = panel.shape[0]
    total[...] = jnp.zeros_like(total)
    place_tiles(swap, 0, 0, coords, live, note, tiles, far, total)
    is_local = near_is_local(swap, lax.axis_index("blk"), lax.axis_index("rep"))

    @pl.when(is_local)
    def _():
        source[...] = panel[...]

    @pl.when(jnp.logical_not(is_local))
    def _():
        source[...] = near[...]

    place_tiles(swap, 1, 0, coords, live, note, tiles, source, total)
    core = lax.rem(lax.axis_index("rep"), 2)
    share = rows // 4
    for h in range(2):
        mine = pl.ds(pl.multiple_of((2 * h + core) * share, share), share)
        other = pl.ds(pl.multiple_of((2 * h + 1 - core) * share, share), share)
        keep[h * share : (h + 1) * share, :] = total[mine, :]
        send[h * share : (h + 1) * share, :] = total[other, :].astype(BF16)


def picked_slot(tiles, picked, sem):
    rep = lax.axis_index("rep")

    @pl.when(swaps_slot(True, lax.axis_index("blk"), rep))
    def _():
        copy = pltpu.make_async_copy(tiles.at[0, 1 - lax.div(rep, 2)], picked, sem)
        copy.start()
        copy.wait()


def prepare(
    swap, tiles, features, cot_own, deg_own, w_self, cot_far, deg_far, *rest,
):
    moved = rest[:-8]
    kept_tiles, panel, self_term, cot, inv_root, deg_near, weights, sems = rest[-8:]
    rep = lax.axis_index("rep")
    core, plane = lax.rem(rep, 2), lax.div(rep, 2)
    share = cot_own.shape[0]
    near = pl.ds(pl.multiple_of(plane * share, share), share)
    away = pl.ds(pl.multiple_of((1 - plane) * share, share), share)
    pairs = [(cot_own, cot.at[near]), (deg_own, deg_near), (w_self, weights), (features, panel)]
    copies = [pltpu.make_async_copy(*pair, sems.at[i]) for i, pair in enumerate(pairs)]
    for copy in copies:
        copy.start()

    tile_copies = []
    for order in range(2):
        is_moved, slot = slot_of(swap, order, rep, lax.axis_index("blk"))
        place = kept_tiles.at[order]
        here = pltpu.make_async_copy(tiles.at[0, slot], place, sems.at[len(tile_copies) + 5])
        tile_copies.append((jnp.logical_not(is_moved), here))
        if moved:
            come = pltpu.make_async_copy(moved[0], place, sems.at[len(tile_copies) + 5])
            tile_copies.append((is_moved, come))
    for is_needed, copy in tile_copies:
        pl.when(is_needed)(copy.start)
    for copy in copies:
        copy.wait()
    cot[away, :] = cot_far[...]
    width = inv_root.shape[1]
    for where, deg in ((near, deg_near[...]), (away, deg_far[:1, :])):
        inv_root[where, :] = jnp.transpose(jnp.broadcast_to(1.0 / jnp.sqrt(deg.astype(F32)), (width, share)))
    for h in range(2):
        rows = panel[pl.ds(pl.multiple_of((2 * h + core) * share, share), share), :]
        self_term[h * share : (h + 1) * share, :] = dot(rows, weights[...], ((1,), (0,)))
    for is_needed, copy in tile_copies:
        pl.when(is_needed)(copy.wait)


def middle(chip_sum, far_sum, inv_root, self_term, cot, panel, w_self, w_neigh, hidden, own_term, message, kept_grad, grads):
    rep = lax.axis_index("rep")
    core, plane = lax.rem(rep, 2), lax.div(rep, 2)
    half, share = chip_sum.shape[0], hidden.shape[0]
    inv = inv_root[...]
    aggregate = ((chip_sum[...] + far_sum[...].astype(F32)) * inv).astype(BF16)
    preact = self_term[...] + dot(aggregate, w_neigh[...], ((1,), (0,)))
    sig = jax.nn.sigmoid(preact)
    slope = sig * (1.0 + preact * (1.0 - sig))
    grad = (cot[...].astype(F32) * slope).astype(BF16)
    message[:half, :] = (dot(grad, w_neigh[...], ((1,), (1,))) * inv).astype(BF16)

    @pl.when(plane == 0)
    def _():
        own = [panel[pl.ds(pl.multiple_of((2 * h + core) * share, share), share), :] for h in range(2)]
        grads[...] = dot(own[0], grad[:share], ((0,), (0,))) + dot(own[1], grad[share:], ((0,), (0,)))

    @pl.when(plane != 0)
    def _():
        grads[...] = dot(aggregate, grad, ((0,), (0,)))

    rows = kept_grad.shape[0]
    kept_grad[...] = grads[pl.ds(pl.multiple_of(core * rows, rows), rows), :]
    message[half:, :] = grads[pl.ds(pl.multiple_of((1 - core) * rows, rows), rows), :].astype(BF16)
    value = (preact * sig).astype(BF16)
    term = dot(grad, w_self[...], ((1,), (1,)))

    @pl.when(plane == 0)
    def _():
        hidden[...] = value[:share]
        own_term[...] = term[:share]

    @pl.when(plane != 0)
    def _():
        hidden[...] = value[share:]
        own_term[...] = term[share:]


def backward(swap, coords, live, note, tiles, own, other, far_cross, far_same, near_first, near_last, source, total):
    rep = lax.axis_index("rep")
    core, plane = lax.rem(rep, 2), lax.div(rep, 2)
    share = source.shape[0] // 4
    for h in range(2):
        part = slice(h * share, (h + 1) * share)
        source[pl.ds(pl.multiple_of((2 * h + core) * share, share), share), :] = own[part, :]
        source[pl.ds(pl.multiple_of((2 * h + 1 - core) * share, share), share), :] = other[part, :]
    half = 2 * share
    same_first = home_first(swap, lax.axis_index("blk"), rep)
    to_plane = jnp.where(same_first, plane, 1 - plane)
    for slot, outs in enumerate(((far_cross, far_same), (near_first, near_last))):
        total[...] = jnp.zeros_like(total)
        place_tiles(swap, slot, 1, coords, live, note, tiles, source, total)
        first = 1 - plane if slot == 0 else to_plane
        for out, which in zip(outs, (first, 1 - first)):
            out[...] = total[pl.ds(pl.multiple_of(which * half, half), half), :].astype(BF16)


def swaps_slot(swap, part, rep):
    return (part % 2 == 0) & (rep % 2 == 0) & swap


def near_is_local(swap, part, rep):
    return rep == (2 * (part % 2) if swap else 2)


def home_first(swap, part, rep):
    return (rep == 2 * (part % 2)) & swap


def kernel_call(kernel, name, outs, args, scratch=(), in_specs=None, out_specs=None):
    return pl.pallas_call(
        kernel,
        out_shape=[jax.ShapeDtypeStruct(*out) for out in outs],
        in_specs=in_specs or [VMEM] * len(args),
        out_specs=out_specs or [VMEM] * len(outs),
        scratch_shapes=scratch,
        compiler_params=pltpu.CompilerParams(vmem_limit_bytes=8 * 2**20),
        name=name,
    )(*args)


def on_device(tile_vals, tile_coords, tile_live, features, degree, w_self, w_neigh, cotangent):
    part_total = lax.axis_size("blk")
    rep_count = lax.axis_size("rep")
    rep = lax.axis_index("rep")
    core, plane = rep % 2, rep // 2
    slots, tile_size = tile_vals.shape[1], tile_vals.shape[3]
    half_span = slots * rep_count // 2
    rows, dim = features.shape
    half, share = rows // 2, rows // rep_count

    swap = part_total == slots * rep_count

    def far(part, r):
        if swap and r == 2 and part % 2 == 0:
            return 1 - half_span
        return slots * r + r // 2 - half_span

    def near(part, r):
        if swap and r in (0, 2) and part % 2 == 0:
            return 0 if r == 0 else 1
        return slots * r + 1 - r // 2 - half_span

    def flip_core(value):
        return exchange(value, lambda b, r: (b, r ^ 1))

    def flip_plane(value):
        return exchange(value, lambda b, r: (b, r ^ 2))

    def fetch(shift):
        pairs = []
        for part in range(part_total):
            for r in range(rep_count):
                if shift(part, r):
                    pairs.append((((part + shift(part, r)) % part_total) * rep_count + r, part * rep_count + r))
        return lax.ppermute(features, BOTH, pairs)

    panel_far, panel_near = fetch(far), fetch(near)

    def note_of(slot):
        parts = [degree, tile_coords[0, slot].reshape(-1), tile_live[0, slot]]
        parts.append(jnp.zeros((2 * share - sum(p.size for p in parts),), jnp.int32))
        return jnp.concatenate(parts)

    far_note = flip_plane(jnp.where(plane == 0, note_of(1), note_of(0)))
    cot_far = flip_plane(cotangent)
    moved = []
    if swap:
        pairs = []
        for part in range(0, part_total, 2):
            pairs += [(part * rep_count, part * rep_count + 2), (part * rep_count + 2, part * rep_count)]
        picked = kernel_call(
            picked_slot, "picked_slot", [(tile_vals.shape[2:], BF16)], [pltpu.with_memory_space_constraint(tile_vals, pltpu.HBM)],
            [pltpu.SemaphoreType.DMA], [pl.BlockSpec(memory_space=pltpu.HBM)],
        )[0]
        moved.append(lax.ppermute(picked, BOTH, pairs))
    wide = (half, dim)
    raw = [tile_vals, features, cotangent, degree.reshape(1, share), w_self]
    raw = [pltpu.with_memory_space_constraint(a, pltpu.HBM) for a in raw]
    tiles, panel, self_term, cot, inv_root = kernel_call(
        functools.partial(prepare, swap),
        "prepare",
        [(tile_vals.shape[1:], BF16), ((rows, dim), BF16), (wide, F32), (wide, BF16), (wide, F32)],
        raw + [cot_far, far_note.reshape(2, share)] + moved,
        [pltpu.VMEM((1, share), jnp.int32), pltpu.VMEM(w_self.shape, BF16), pltpu.SemaphoreType.DMA((7 + 2 * len(moved),))],
        [pl.BlockSpec(memory_space=pltpu.HBM)] * 5 + [VMEM] * 2 + [pl.BlockSpec(memory_space=pl.ANY)] * len(moved),
    )

    source, total = pltpu.VMEM((rows, dim), BF16), pltpu.VMEM((rows + tile_size, dim), F32)
    scalars = [tile_coords.transpose(0, 1, 3, 2), tile_live, far_note]
    keep, send = kernel_call(
        functools.partial(forward, swap), "forward", [(wide, F32), (wide, BF16)], scalars + [tiles, panel_far, panel_near, panel],
        [source, total], [SMEM] * 3 + [VMEM] * 4,
    )
    chip_sum = keep + flip_core(send).astype(F32)
    far_sum = flip_plane(chip_sum.astype(BF16))

    grad_rows = dim // 2
    hidden, own_term, message, kept_grad = kernel_call(
        middle,
        "middle",
        [((share, dim), BF16), ((share, dim), F32), ((half + grad_rows, dim), BF16), ((grad_rows, dim), F32)],
        [chip_sum, far_sum, inv_root, self_term, cot, panel, w_self, w_neigh],
        [pltpu.VMEM((dim, dim), F32)],
    )
    other = flip_core(message)
    sends = kernel_call(
        functools.partial(backward, swap), "backward", [(wide, BF16)] * 4, scalars + [tiles, message, other], [source, total],
        [SMEM] * 3 + [VMEM] * 3,
    )

    def others(value, bit, rep_bit=0):
        return exchange(value, lambda b, r: (b ^ bit, r ^ rep_bit))

    def added(one, two):
        return (one.astype(F32) + two.astype(F32)).astype(BF16)

    def tied(value, *after):
        return lax.optimization_barrier((value,) + after)[0]

    sends = list(sends)
    rounded = (kept_grad + other[half:].astype(F32)).astype(BF16)
    top = part_total.bit_length() - 2
    def near_first(part, r, flip):
        return (part + near(part, r), r if bool(home_first(swap, part, r)) != flip else r ^ 2)

    arrived = [
        exchange(sends[0], lambda b, r: (b + far(b, r), r ^ 2)),
        exchange(sends[1], lambda b, r: (b + far(b, r), r)),
        exchange(sends[2], lambda b, r: near_first(b, r, False)),
        exchange(sends[3], lambda b, r: near_first(b, r, True)),
    ]

    rounded = added(rounded, tied(others(rounded, 1 << top), sends[0]))
    rounded = added(rounded, tied(others(rounded, 2), arrived[0]))
    rounded = added(rounded, tied(others(rounded, 1), arrived[1]))
    twin = flip_plane(rounded)
    by_plane = jnp.where(plane == 0, jnp.stack([rounded, twin]), jnp.stack([twin, rounded]))
    twin = flip_core(by_plane)
    by_core = jnp.where(core == 0, jnp.stack([by_plane, twin], 1), jnp.stack([twin, by_plane], 1))
    grad_scale = 1.0 / math.sqrt(rows * part_total)
    totals = by_core.reshape(2, dim, dim).astype(F32) * grad_scale

    neighbour = sum(a.astype(F32) for a in arrived).reshape(2, share, dim)
    twin = flip_core(lax.dynamic_index_in_dim(neighbour, 1 - core, 0, keepdims=False).astype(BF16))
    neighbour = lax.dynamic_index_in_dim(neighbour, core, 0, keepdims=False) + twin.astype(F32)
    grad_features = (own_term + neighbour).astype(BF16)
    return (hidden, grad_features, totals[0], totals[1])


def solution(mesh):
    return jax.shard_map(
        on_device,
        mesh=mesh,
        in_specs=(
            P("blk", "rep", None, None, None),
            P("blk", "rep", None, None),
            P("blk", "rep", None),
            P("blk", None),
            P(("blk", "rep")),
            P(),
            P(),
            P(("blk", "rep"), None),
        ),
        out_specs=(P(("blk", "rep"), None), P(("blk", "rep"), None), P(), P()),
        check_vma=False,
    )
```

```python
import functools
import math

import jax
import jax.numpy as jnp
from jax import lax
from jax.experimental import pallas as pl
from jax.experimental.pallas import tpu as pltpu
from jax.sharding import PartitionSpec as P

BOTH = ("blk", "rep")
BF16 = jnp.bfloat16
F32 = jnp.float32
VMEM = pl.BlockSpec(memory_space=pltpu.VMEM)
SMEM = pl.BlockSpec(memory_space=pltpu.SMEM)


def exchange(value, target):
    part_total, rep_count = lax.axis_size("blk"), lax.axis_size("rep")
    pairs = []
    for part in range(part_total):
        for rep in range(rep_count):
            to_part, to_rep = target(part, rep)
            pairs.append((part * rep_count + rep, (to_part % part_total) * rep_count + to_rep))
    return lax.ppermute(value, BOTH, pairs)


def dot(lhs, rhs, contract):
    return lax.dot_general(lhs, rhs, (contract, ((), ())), preferred_element_type=F32)


def slot_of(swap, order, rep, part):
    plane = lax.div(rep, 2)
    swaps = swaps_slot(swap, part, rep)
    moved = jnp.logical_and(swaps, plane == 1 - order)
    if order == 0:
        return moved, plane
    return moved, jnp.where(jnp.logical_and(swaps, plane == 1), 1, 1 - plane)


def place_tiles(swap, order, out_axis, coords, live, note, tiles, source, total):
    size, tile_count = tiles.shape[-1], tiles.shape[-3]
    spare = total.shape[0] // size - 1
    moved, slot = slot_of(swap, order, lax.axis_index("rep"), lax.axis_index("blk"))
    at = note.shape[0] // 2
    for k in range(tile_count):
        places = [jnp.where(moved, note[at + 2 * k + axis], coords[0, slot, axis, k]) for axis in range(2)]
        present = jnp.where(moved, note[at + 2 * tile_count + k], live[0, slot, k]) != 0
        take, to = places[1 - out_axis], jnp.where(present, places[out_axis], spare)
        block = source[pl.ds(pl.multiple_of(take * size, size), size), :]
        rows = pl.ds(pl.multiple_of(to * size, size), size)
        total[rows, :] += dot(tiles[order, k], block, ((1 - out_axis,), (0,)))


def forward(swap, coords, live, note, tiles, far, near, panel, keep, send, source, total):
    rows = panel.shape[0]
    total[...] = jnp.zeros_like(total)
    place_tiles(swap, 0, 0, coords, live, note, tiles, far, total)
    is_local = near_is_local(swap, lax.axis_index("blk"), lax.axis_index("rep"))

    @pl.when(is_local)
    def _():
        source[...] = panel[...]

    @pl.when(jnp.logical_not(is_local))
    def _():
        source[...] = near[...]

    place_tiles(swap, 1, 0, coords, live, note, tiles, source, total)
    core = lax.rem(lax.axis_index("rep"), 2)
    share = rows // 4
    for h in range(2):
        mine = pl.ds(pl.multiple_of((2 * h + core) * share, share), share)
        other = pl.ds(pl.multiple_of((2 * h + 1 - core) * share, share), share)
        keep[h * share : (h + 1) * share, :] = total[mine, :]
        send[h * share : (h + 1) * share, :] = total[other, :].astype(BF16)


def picked_slot(tiles, picked, sem):
    rep = lax.axis_index("rep")

    @pl.when(swaps_slot(True, lax.axis_index("blk"), rep))
    def _():
        copy = pltpu.make_async_copy(tiles.at[0, 1 - lax.div(rep, 2)], picked, sem)
        copy.start()
        copy.wait()


def prepare(
    swap, tiles, features, cot_own, deg_own, w_self, cot_far, deg_far, *rest,
):
    moved = rest[:-8]
    kept_tiles, panel, self_term, cot, inv_root, deg_near, weights, sems = rest[-8:]
    rep = lax.axis_index("rep")
    core, plane = lax.rem(rep, 2), lax.div(rep, 2)
    share = cot_own.shape[0]
    near = pl.ds(pl.multiple_of(plane * share, share), share)
    away = pl.ds(pl.multiple_of((1 - plane) * share, share), share)
    pairs = [(cot_own, cot.at[near]), (deg_own, deg_near), (w_self, weights), (features, panel)]
    copies = [pltpu.make_async_copy(*pair, sems.at[i]) for i, pair in enumerate(pairs)]
    for copy in copies:
        copy.start()

    tile_copies = []
    for order in range(2):
        is_moved, slot = slot_of(swap, order, rep, lax.axis_index("blk"))
        place = kept_tiles.at[order]
        here = pltpu.make_async_copy(tiles.at[0, slot], place, sems.at[len(tile_copies) + 5])
        tile_copies.append((jnp.logical_not(is_moved), here))
        if moved:
            come = pltpu.make_async_copy(moved[0], place, sems.at[len(tile_copies) + 5])
            tile_copies.append((is_moved, come))
    for is_needed, copy in tile_copies:
        pl.when(is_needed)(copy.start)
    for copy in copies:
        copy.wait()
    cot[away, :] = cot_far[...]
    width = inv_root.shape[1]
    for where, deg in ((near, deg_near[...]), (away, deg_far[:1, :])):
        inv_root[where, :] = jnp.transpose(jnp.broadcast_to(1.0 / jnp.sqrt(deg.astype(F32)), (width, share)))
    for h in range(2):
        rows = panel[pl.ds(pl.multiple_of((2 * h + core) * share, share), share), :]
        self_term[h * share : (h + 1) * share, :] = dot(rows, weights[...], ((1,), (0,)))
    for is_needed, copy in tile_copies:
        pl.when(is_needed)(copy.wait)


def middle(chip_sum, far_sum, inv_root, self_term, cot, panel, w_self, w_neigh, hidden, own_term, message, kept_grad, grads):
    rep = lax.axis_index("rep")
    core, plane = lax.rem(rep, 2), lax.div(rep, 2)
    half, share = chip_sum.shape[0], hidden.shape[0]
    inv = inv_root[...]
    aggregate = ((chip_sum[...] + far_sum[...].astype(F32)) * inv).astype(BF16)
    preact = self_term[...] + dot(aggregate, w_neigh[...], ((1,), (0,)))
    sig = jax.nn.sigmoid(preact)
    slope = sig * (1.0 + preact * (1.0 - sig))
    grad = (cot[...].astype(F32) * slope).astype(BF16)
    message[:half, :] = (dot(grad, w_neigh[...], ((1,), (1,))) * inv).astype(BF16)
    own = [panel[pl.ds(pl.multiple_of((2 * h + core) * share, share), share), :] for h in range(2)]
    left = jnp.where(plane == 0, jnp.concatenate(own).astype(F32), aggregate.astype(F32)).astype(BF16)
    grads[...] = dot(left, grad, ((0,), (0,)))
    rows = kept_grad.shape[0]
    kept_grad[...] = grads[pl.ds(pl.multiple_of(core * rows, rows), rows), :]
    message[half:, :] = grads[pl.ds(pl.multiple_of((1 - core) * rows, rows), rows), :].astype(BF16)
    value = (preact * sig).astype(BF16)
    term = dot(grad, w_self[...], ((1,), (1,)))

    @pl.when(plane == 0)
    def _():
        hidden[...] = value[:share]
        own_term[...] = term[:share]

    @pl.when(plane != 0)
    def _():
        hidden[...] = value[share:]
        own_term[...] = term[share:]


def backward(swap, coords, live, note, tiles, own, other, far_cross, far_same, near_first, near_last, source, total):
    rep = lax.axis_index("rep")
    core, plane = lax.rem(rep, 2), lax.div(rep, 2)
    share = source.shape[0] // 4
    for h in range(2):
        part = slice(h * share, (h + 1) * share)
        source[pl.ds(pl.multiple_of((2 * h + core) * share, share), share), :] = own[part, :]
        source[pl.ds(pl.multiple_of((2 * h + 1 - core) * share, share), share), :] = other[part, :]
    half = 2 * share
    same_first = home_first(swap, lax.axis_index("blk"), rep)
    to_plane = jnp.where(same_first, plane, 1 - plane)
    for slot, outs in enumerate(((far_cross, far_same), (near_first, near_last))):
        total[...] = jnp.zeros_like(total)
        place_tiles(swap, slot, 1, coords, live, note, tiles, source, total)
        first = 1 - plane if slot == 0 else to_plane
        for out, which in zip(outs, (first, 1 - first)):
            out[...] = total[pl.ds(pl.multiple_of(which * half, half), half), :].astype(BF16)


def swaps_slot(swap, part, rep):
    return (part % 2 == 0) & (rep % 2 == 0) & swap


def near_is_local(swap, part, rep):
    return rep == (2 * (part % 2) if swap else 2)


def home_first(swap, part, rep):
    return (rep == 2 * (part % 2)) & swap


def kernel_call(kernel, name, outs, args, scratch=(), in_specs=None, out_specs=None):
    return pl.pallas_call(
        kernel,
        out_shape=[jax.ShapeDtypeStruct(*out) for out in outs],
        in_specs=in_specs or [VMEM] * len(args),
        out_specs=out_specs or [VMEM] * len(outs),
        scratch_shapes=scratch,
        compiler_params=pltpu.CompilerParams(vmem_limit_bytes=8 * 2**20),
        name=name,
    )(*args)


def on_device(tile_vals, tile_coords, tile_live, features, degree, w_self, w_neigh, cotangent):
    part_total = lax.axis_size("blk")
    rep_count = lax.axis_size("rep")
    rep = lax.axis_index("rep")
    core, plane = rep % 2, rep // 2
    slots, tile_size = tile_vals.shape[1], tile_vals.shape[3]
    half_span = slots * rep_count // 2
    rows, dim = features.shape
    half, share = rows // 2, rows // rep_count

    swap = part_total == slots * rep_count

    def far(part, r):
        if swap and r == 2 and part % 2 == 0:
            return 1 - half_span
        return slots * r + r // 2 - half_span

    def near(part, r):
        if swap and r in (0, 2) and part % 2 == 0:
            return 0 if r == 0 else 1
        return slots * r + 1 - r // 2 - half_span

    def flip_core(value):
        return exchange(value, lambda b, r: (b, r ^ 1))

    def flip_plane(value):
        return exchange(value, lambda b, r: (b, r ^ 2))

    def fetch(shift):
        pairs = []
        for part in range(part_total):
            for r in range(rep_count):
                if shift(part, r):
                    pairs.append((((part + shift(part, r)) % part_total) * rep_count + r, part * rep_count + r))
        return lax.ppermute(features, BOTH, pairs)

    panel_far, panel_near = fetch(far), fetch(near)

    def note_of(slot):
        parts = [degree, tile_coords[0, slot].reshape(-1), tile_live[0, slot]]
        parts.append(jnp.zeros((2 * share - sum(p.size for p in parts),), jnp.int32))
        return jnp.concatenate(parts)

    far_note = flip_plane(jnp.where(plane == 0, note_of(1), note_of(0)))
    cot_far = flip_plane(cotangent)
    moved = []
    if swap:
        pairs = []
        for part in range(0, part_total, 2):
            pairs += [(part * rep_count, part * rep_count + 2), (part * rep_count + 2, part * rep_count)]
        picked = kernel_call(
            picked_slot, "picked_slot", [(tile_vals.shape[2:], BF16)], [pltpu.with_memory_space_constraint(tile_vals, pltpu.HBM)],
            [pltpu.SemaphoreType.DMA], [pl.BlockSpec(memory_space=pltpu.HBM)],
        )[0]
        moved.append(lax.ppermute(picked, BOTH, pairs))
    wide = (half, dim)
    raw = [tile_vals, features, cotangent, degree.reshape(1, share), w_self]
    raw = [pltpu.with_memory_space_constraint(a, pltpu.HBM) for a in raw]
    tiles, panel, self_term, cot, inv_root = kernel_call(
        functools.partial(prepare, swap),
        "prepare",
        [(tile_vals.shape[1:], BF16), ((rows, dim), BF16), (wide, F32), (wide, BF16), (wide, F32)],
        raw + [cot_far, far_note.reshape(2, share)] + moved,
        [pltpu.VMEM((1, share), jnp.int32), pltpu.VMEM(w_self.shape, BF16), pltpu.SemaphoreType.DMA((7 + 2 * len(moved),))],
        [pl.BlockSpec(memory_space=pltpu.HBM)] * 5 + [VMEM] * 2 + [pl.BlockSpec(memory_space=pl.ANY)] * len(moved),
    )

    source, total = pltpu.VMEM((rows, dim), BF16), pltpu.VMEM((rows + tile_size, dim), F32)
    scalars = [tile_coords.transpose(0, 1, 3, 2), tile_live, far_note]
    keep, send = kernel_call(
        functools.partial(forward, swap), "forward", [(wide, F32), (wide, BF16)], scalars + [tiles, panel_far, panel_near, panel],
        [source, total], [SMEM] * 3 + [VMEM] * 4,
    )
    chip_sum = keep + flip_core(send).astype(F32)
    far_sum = flip_plane(chip_sum.astype(BF16))

    grad_rows = dim // 2
    hidden, own_term, message, kept_grad = kernel_call(
        middle,
        "middle",
        [((share, dim), BF16), ((share, dim), F32), ((half + grad_rows, dim), BF16), ((grad_rows, dim), F32)],
        [chip_sum, far_sum, inv_root, self_term, cot, panel, w_self, w_neigh],
        [pltpu.VMEM((dim, dim), F32)],
    )
    other = flip_core(message)
    sends = kernel_call(
        functools.partial(backward, swap), "backward", [(wide, BF16)] * 4, scalars + [tiles, message, other], [source, total],
        [SMEM] * 3 + [VMEM] * 3,
    )

    def others(value, bit, rep_bit=0):
        return exchange(value, lambda b, r: (b ^ bit, r ^ rep_bit))

    def added(one, two):
        return (one.astype(F32) + two.astype(F32)).astype(BF16)

    def tied(value, *after):
        return lax.optimization_barrier((value,) + after)[0]

    sends = list(sends)
    rounded = (kept_grad + other[half:].astype(F32)).astype(BF16)
    top = part_total.bit_length() - 2
    def near_first(part, r, flip):
        return (part + near(part, r), r if bool(home_first(swap, part, r)) != flip else r ^ 2)

    arrived = [
        exchange(sends[0], lambda b, r: (b + far(b, r), r ^ 2)),
        exchange(sends[1], lambda b, r: (b + far(b, r), r)),
        exchange(sends[2], lambda b, r: near_first(b, r, False)),
        exchange(sends[3], lambda b, r: near_first(b, r, True)),
    ]

    rounded = added(rounded, tied(others(rounded, 1 << top), sends[0]))
    rounded = added(rounded, tied(others(rounded, 2), arrived[0]))
    rounded = added(rounded, tied(others(rounded, 1), arrived[1]))
    twin = flip_plane(rounded)
    by_plane = jnp.where(plane == 0, jnp.stack([rounded, twin]), jnp.stack([twin, rounded]))
    twin = flip_core(by_plane)
    by_core = jnp.where(core == 0, jnp.stack([by_plane, twin], 1), jnp.stack([twin, by_plane], 1))
    grad_scale = 1.0 / math.sqrt(rows * part_total)
    totals = by_core.reshape(2, dim, dim).astype(F32) * grad_scale

    neighbour = sum(a.astype(F32) for a in arrived).reshape(2, share, dim)
    twin = flip_core(lax.dynamic_index_in_dim(neighbour, 1 - core, 0, keepdims=False).astype(BF16))
    neighbour = lax.dynamic_index_in_dim(neighbour, core, 0, keepdims=False) + twin.astype(F32)
    grad_features = (own_term + neighbour).astype(BF16)
    return (hidden, grad_features, totals[0], totals[1])


def solution(mesh):
    return jax.shard_map(
        on_device,
        mesh=mesh,
        in_specs=(
            P("blk", "rep", None, None, None),
            P("blk", "rep", None, None),
            P("blk", "rep", None),
            P("blk", None),
            P(("blk", "rep")),
            P(),
            P(),
            P(("blk", "rep"), None),
        ),
        out_specs=(P(("blk", "rep"), None), P(("blk", "rep"), None), P(), P()),
        check_vma=False,
    )
```

```python
import functools
import math

import jax
import jax.numpy as jnp
from jax import lax
from jax.experimental import pallas as pl
from jax.experimental.pallas import tpu as pltpu
from jax.sharding import PartitionSpec as P

BOTH = ("blk", "rep")
BF16 = jnp.bfloat16
F32 = jnp.float32
VMEM = pl.BlockSpec(memory_space=pltpu.VMEM)
SMEM = pl.BlockSpec(memory_space=pltpu.SMEM)


def exchange(value, target):
    part_total, rep_count = lax.axis_size("blk"), lax.axis_size("rep")
    pairs = []
    for part in range(part_total):
        for rep in range(rep_count):
            to_part, to_rep = target(part, rep)
            pairs.append((part * rep_count + rep, (to_part % part_total) * rep_count + to_rep))
    return lax.ppermute(value, BOTH, pairs)


def dot(lhs, rhs, contract):
    return lax.dot_general(lhs, rhs, (contract, ((), ())), preferred_element_type=F32)


def slot_of(swap, order, rep, part):
    plane = lax.div(rep, 2)
    swaps = swaps_slot(swap, part, rep)
    moved = jnp.logical_and(swaps, plane == 1 - order)
    if order == 0:
        return moved, plane
    return moved, jnp.where(jnp.logical_and(swaps, plane == 1), 1, 1 - plane)


def place_tiles(swap, order, out_axis, coords, live, note, tiles, source, total):
    size, tile_count = tiles.shape[-1], tiles.shape[-3]
    spare = total.shape[0] // size - 1
    moved, slot = slot_of(swap, order, lax.axis_index("rep"), lax.axis_index("blk"))
    at = note.shape[0] // 2
    for k in range(tile_count):
        places = [jnp.where(moved, note[at + 2 * k + axis], coords[0, slot, axis, k]) for axis in range(2)]
        present = jnp.where(moved, note[at + 2 * tile_count + k], live[0, slot, k]) != 0
        take, to = places[1 - out_axis], jnp.where(present, places[out_axis], spare)
        block = source[pl.ds(pl.multiple_of(take * size, size), size), :]
        rows = pl.ds(pl.multiple_of(to * size, size), size)
        total[rows, :] += dot(tiles[order, k], block, ((1 - out_axis,), (0,)))


def forward(swap, coords, live, note, tiles, far, near, panel, keep, send, source, total):
    rows = panel.shape[0]
    total[...] = jnp.zeros_like(total)
    place_tiles(swap, 0, 0, coords, live, note, tiles, far, total)
    is_local = near_is_local(swap, lax.axis_index("blk"), lax.axis_index("rep"))

    @pl.when(is_local)
    def _():
        source[...] = panel[...]

    @pl.when(jnp.logical_not(is_local))
    def _():
        source[...] = near[...]

    place_tiles(swap, 1, 0, coords, live, note, tiles, source, total)
    core = lax.rem(lax.axis_index("rep"), 2)
    share = rows // 4
    for h in range(2):
        mine = pl.ds(pl.multiple_of((2 * h + core) * share, share), share)
        other = pl.ds(pl.multiple_of((2 * h + 1 - core) * share, share), share)
        keep[h * share : (h + 1) * share, :] = total[mine, :]
        send[h * share : (h + 1) * share, :] = total[other, :].astype(BF16)


def picked_slot(tiles, picked, sem):
    rep = lax.axis_index("rep")

    @pl.when(swaps_slot(True, lax.axis_index("blk"), rep))
    def _():
        copy = pltpu.make_async_copy(tiles.at[0, 1 - lax.div(rep, 2)], picked, sem)
        copy.start()
        copy.wait()


def prepare(
    swap, tiles, features, cot_own, deg_own, w_self, cot_far, deg_far, *rest,
):
    moved = rest[:-8]
    kept_tiles, panel, self_term, cot, inv_root, deg_near, weights, sems = rest[-8:]
    rep = lax.axis_index("rep")
    core, plane = lax.rem(rep, 2), lax.div(rep, 2)
    share = cot_own.shape[0]
    near = pl.ds(pl.multiple_of(plane * share, share), share)
    away = pl.ds(pl.multiple_of((1 - plane) * share, share), share)
    pairs = [(cot_own, cot.at[near]), (deg_own, deg_near), (w_self, weights), (features, panel)]
    copies = [pltpu.make_async_copy(*pair, sems.at[i]) for i, pair in enumerate(pairs)]
    for copy in copies:
        copy.start()

    tile_copies = []
    for order in range(2):
        is_moved, slot = slot_of(swap, order, rep, lax.axis_index("blk"))
        place = kept_tiles.at[order]
        here = pltpu.make_async_copy(tiles.at[0, slot], place, sems.at[len(tile_copies) + 5])
        tile_copies.append((jnp.logical_not(is_moved), here))
        if moved:
            come = pltpu.make_async_copy(moved[0], place, sems.at[len(tile_copies) + 5])
            tile_copies.append((is_moved, come))
    for is_needed, copy in tile_copies:
        pl.when(is_needed)(copy.start)
    for copy in copies:
        copy.wait()
    cot[away, :] = cot_far[...]
    width = inv_root.shape[1]
    for where, deg in ((near, deg_near[...]), (away, deg_far[:1, :])):
        inv_root[where, :] = jnp.transpose(jnp.broadcast_to(1.0 / jnp.sqrt(deg.astype(F32)), (width, share)))
    for h in range(2):
        rows = panel[pl.ds(pl.multiple_of((2 * h + core) * share, share), share), :]
        self_term[h * share : (h + 1) * share, :] = dot(rows, weights[...], ((1,), (0,)))
    for is_needed, copy in tile_copies:
        pl.when(is_needed)(copy.wait)


def middle(chip_sum, far_sum, inv_root, self_term, cot, panel, w_self, w_neigh, hidden, own_term, message, kept_grad, grads):
    rep = lax.axis_index("rep")
    core, plane = lax.rem(rep, 2), lax.div(rep, 2)
    half, share = chip_sum.shape[0], hidden.shape[0]
    inv = inv_root[...]
    aggregate = ((chip_sum[...] + far_sum[...].astype(F32)) * inv).astype(BF16)
    preact = self_term[...] + dot(aggregate, w_neigh[...], ((1,), (0,)))
    sig = jax.nn.sigmoid(preact)
    slope = sig * (1.0 + preact * (1.0 - sig))
    grad = (cot[...].astype(F32) * slope).astype(BF16)
    message[:half, :] = (dot(grad, w_neigh[...], ((1,), (1,))) * inv).astype(BF16)
    own = [panel[pl.ds(pl.multiple_of((2 * h + core) * share, share), share), :] for h in range(2)]
    left = jnp.where(plane == 0, jnp.concatenate(own).astype(F32), aggregate.astype(F32)).astype(BF16)
    grads[...] = dot(left, grad, ((0,), (0,)))
    rows = kept_grad.shape[0]
    kept_grad[...] = grads[pl.ds(pl.multiple_of(core * rows, rows), rows), :]
    message[half:, :] = grads[pl.ds(pl.multiple_of((1 - core) * rows, rows), rows), :].astype(BF16)
    value = (preact * sig).astype(BF16)
    term = dot(grad, w_self[...], ((1,), (1,)))

    @pl.when(plane == 0)
    def _():
        hidden[...] = value[:share]
        own_term[...] = term[:share]

    @pl.when(plane != 0)
    def _():
        hidden[...] = value[share:]
        own_term[...] = term[share:]


def backward(swap, coords, live, note, tiles, own, other, far_cross, far_same, near_first, near_last, source, total):
    rep = lax.axis_index("rep")
    core, plane = lax.rem(rep, 2), lax.div(rep, 2)
    share = source.shape[0] // 4
    for h in range(2):
        part = slice(h * share, (h + 1) * share)
        source[pl.ds(pl.multiple_of((2 * h + core) * share, share), share), :] = own[part, :]
        source[pl.ds(pl.multiple_of((2 * h + 1 - core) * share, share), share), :] = other[part, :]
    half = 2 * share
    same_first = home_first(swap, lax.axis_index("blk"), rep)
    to_plane = jnp.where(same_first, plane, 1 - plane)
    for slot, outs in enumerate(((far_cross, far_same), (near_first, near_last))):
        total[...] = jnp.zeros_like(total)
        place_tiles(swap, slot, 1, coords, live, note, tiles, source, total)
        first = 1 - plane if slot == 0 else to_plane
        for out, which in zip(outs, (first, 1 - first)):
            out[...] = total[pl.ds(pl.multiple_of(which * half, half), half), :].astype(BF16)


def swaps_slot(swap, part, rep):
    return (part % 2 == 0) & (rep % 2 == 0) & swap


def near_is_local(swap, part, rep):
    return rep == (2 * (part % 2) if swap else 2)


def home_first(swap, part, rep):
    return (rep == 2 * (part % 2)) & swap


def kernel_call(kernel, name, outs, args, scratch=(), in_specs=None, out_specs=None):
    return pl.pallas_call(
        kernel,
        out_shape=[jax.ShapeDtypeStruct(*out) for out in outs],
        in_specs=in_specs or [VMEM] * len(args),
        out_specs=out_specs or [VMEM] * len(outs),
        scratch_shapes=scratch,
        compiler_params=pltpu.CompilerParams(vmem_limit_bytes=8 * 2**20),
        name=name,
    )(*args)


def on_device(tile_vals, tile_coords, tile_live, features, degree, w_self, w_neigh, cotangent):
    part_total = lax.axis_size("blk")
    rep_count = lax.axis_size("rep")
    rep = lax.axis_index("rep")
    core, plane = rep % 2, rep // 2
    slots, tile_size = tile_vals.shape[1], tile_vals.shape[3]
    half_span = slots * rep_count // 2
    rows, dim = features.shape
    half, share = rows // 2, rows // rep_count

    swap = part_total == slots * rep_count

    def far(part, r):
        if swap and r == 2 and part % 2 == 0:
            return 1 - half_span
        return slots * r + r // 2 - half_span

    def near(part, r):
        if swap and r in (0, 2) and part % 2 == 0:
            return 0 if r == 0 else 1
        return slots * r + 1 - r // 2 - half_span

    def flip_core(value):
        return exchange(value, lambda b, r: (b, r ^ 1))

    def flip_plane(value):
        return exchange(value, lambda b, r: (b, r ^ 2))

    def fetch(shift):
        pairs = []
        for part in range(part_total):
            for r in range(rep_count):
                if shift(part, r):
                    pairs.append((((part + shift(part, r)) % part_total) * rep_count + r, part * rep_count + r))
        return lax.ppermute(features, BOTH, pairs)

    panel_far, panel_near = fetch(far), fetch(near)

    def note_of(slot):
        parts = [degree, tile_coords[0, slot].reshape(-1), tile_live[0, slot]]
        parts.append(jnp.zeros((2 * share - sum(p.size for p in parts),), jnp.int32))
        return jnp.concatenate(parts)

    far_note = flip_plane(jnp.where(plane == 0, note_of(1), note_of(0)))
    cot_far = flip_plane(cotangent)
    moved = []
    if swap:
        pairs = []
        for part in range(0, part_total, 2):
            pairs += [(part * rep_count, part * rep_count + 2), (part * rep_count + 2, part * rep_count)]
        picked = kernel_call(
            picked_slot, "picked_slot", [(tile_vals.shape[2:], BF16)], [pltpu.with_memory_space_constraint(tile_vals, pltpu.HBM)],
            [pltpu.SemaphoreType.DMA], [pl.BlockSpec(memory_space=pltpu.HBM)],
        )[0]
        moved.append(lax.ppermute(picked, BOTH, pairs))
    wide = (half, dim)
    raw = [tile_vals, features, cotangent, degree.reshape(1, share), w_self]
    raw = [pltpu.with_memory_space_constraint(a, pltpu.HBM) for a in raw]
    tiles, panel, self_term, cot, inv_root = kernel_call(
        functools.partial(prepare, swap),
        "prepare",
        [(tile_vals.shape[1:], BF16), ((rows, dim), BF16), (wide, F32), (wide, BF16), (wide, F32)],
        raw + [cot_far, far_note.reshape(2, share)] + moved,
        [pltpu.VMEM((1, share), jnp.int32), pltpu.VMEM(w_self.shape, BF16), pltpu.SemaphoreType.DMA((7 + 2 * len(moved),))],
        [pl.BlockSpec(memory_space=pltpu.HBM)] * 5 + [VMEM] * 2 + [pl.BlockSpec(memory_space=pl.ANY)] * len(moved),
    )

    source, total = pltpu.VMEM((rows, dim), BF16), pltpu.VMEM((rows + tile_size, dim), F32)
    scalars = [tile_coords.transpose(0, 1, 3, 2), tile_live, far_note]
    keep, send = kernel_call(
        functools.partial(forward, swap), "forward", [(wide, F32), (wide, BF16)], scalars + [tiles, panel_far, panel_near, panel],
        [source, total], [SMEM] * 3 + [VMEM] * 4,
    )
    chip_sum = keep + flip_core(send).astype(F32)
    far_sum = flip_plane(chip_sum.astype(BF16))

    grad_rows = dim // 2
    hidden, own_term, message, kept_grad = kernel_call(
        middle,
        "middle",
        [((share, dim), BF16), ((share, dim), F32), ((half + grad_rows, dim), BF16), ((grad_rows, dim), F32)],
        [chip_sum, far_sum, inv_root, self_term, cot, panel, w_self, w_neigh],
        [pltpu.VMEM((dim, dim), F32)],
    )
    other = flip_core(message)
    sends = kernel_call(
        functools.partial(backward, swap), "backward", [(wide, BF16)] * 4, scalars + [tiles, message, other], [source, total],
        [SMEM] * 3 + [VMEM] * 3,
    )

    def others(value, bit, rep_bit=0):
        return exchange(value, lambda b, r: (b ^ bit, r ^ rep_bit))

    def added(one, two):
        return (one.astype(F32) + two.astype(F32)).astype(BF16)

    def tied(value, *after):
        return lax.optimization_barrier((value,) + after)[0]

    sends = list(sends)
    rounded = (kept_grad + other[half:].astype(F32)).astype(BF16)
    top = part_total.bit_length() - 2
    def near_first(part, r, flip):
        return (part + near(part, r), r if bool(home_first(swap, part, r)) != flip else r ^ 2)

    arrived = [
        exchange(sends[0], lambda b, r: (b + far(b, r), r ^ 2)),
        exchange(sends[1], lambda b, r: (b + far(b, r), r)),
        exchange(sends[2], lambda b, r: near_first(b, r, False)),
        exchange(sends[3], lambda b, r: near_first(b, r, True)),
    ]

    rounded = added(rounded, tied(others(rounded, 1 << top), sends[0]))
    for i in range(top - 1, 1, -1):
        rounded = added(rounded, others(rounded, 1 << i))
    rounded = added(rounded, tied(others(rounded, 2), arrived[0]))
    rounded = added(rounded, tied(others(rounded, 1), arrived[1]))
    twin = flip_plane(rounded)
    by_plane = jnp.where(plane == 0, jnp.stack([rounded, twin]), jnp.stack([twin, rounded]))
    twin = flip_core(by_plane)
    by_core = jnp.where(core == 0, jnp.stack([by_plane, twin], 1), jnp.stack([twin, by_plane], 1))
    grad_scale = 1.0 / math.sqrt(rows * part_total)
    totals = by_core.reshape(2, dim, dim).astype(F32) * grad_scale

    neighbour = sum(a.astype(F32) for a in arrived).reshape(2, share, dim)
    twin = flip_core(lax.dynamic_index_in_dim(neighbour, 1 - core, 0, keepdims=False).astype(BF16))
    neighbour = lax.dynamic_index_in_dim(neighbour, core, 0, keepdims=False) + twin.astype(F32)
    grad_features = (own_term + neighbour).astype(BF16)
    return (hidden, grad_features, totals[0], totals[1])


def solution(mesh):
    return jax.shard_map(
        on_device,
        mesh=mesh,
        in_specs=(
            P("blk", "rep", None, None, None),
            P("blk", "rep", None, None),
            P("blk", "rep", None),
            P("blk", None),
            P(("blk", "rep")),
            P(),
            P(),
            P(("blk", "rep"), None),
        ),
        out_specs=(P(("blk", "rep"), None), P(("blk", "rep"), None), P(), P()),
        check_vma=False,
    )
```

```python
import functools
import math

import jax
import jax.numpy as jnp
from jax import lax
from jax.experimental import pallas as pl
from jax.experimental.pallas import tpu as pltpu
from jax.sharding import PartitionSpec as P

BOTH = ("blk", "rep")
BF16 = jnp.bfloat16
F32 = jnp.float32
VMEM = pl.BlockSpec(memory_space=pltpu.VMEM)
SMEM = pl.BlockSpec(memory_space=pltpu.SMEM)


def exchange(value, target):
    part_total, rep_count = lax.axis_size("blk"), lax.axis_size("rep")
    pairs = []
    for part in range(part_total):
        for rep in range(rep_count):
            to_part, to_rep = target(part, rep)
            pairs.append((part * rep_count + rep, (to_part % part_total) * rep_count + to_rep))
    return lax.ppermute(value, BOTH, pairs)


def dot(lhs, rhs, contract):
    return lax.dot_general(lhs, rhs, (contract, ((), ())), preferred_element_type=F32)


def slot_of(swap, order, rep, part):
    plane = lax.div(rep, 2)
    swaps = swaps_slot(swap, part, rep)
    moved = jnp.logical_and(swaps, plane == 1 - order)
    if order == 0:
        return moved, plane
    return moved, jnp.where(jnp.logical_and(swaps, plane == 1), 1, 1 - plane)


def place_tiles(swap, order, out_axis, coords, live, note, tiles, source, total):
    size, tile_count = tiles.shape[-1], tiles.shape[-3]
    spare = total.shape[0] // size - 1
    moved, slot = slot_of(swap, order, lax.axis_index("rep"), lax.axis_index("blk"))
    at = note.shape[0] // 2
    for k in range(tile_count):
        places = [jnp.where(moved, note[at + 2 * k + axis], coords[0, slot, axis, k]) for axis in range(2)]
        present = jnp.where(moved, note[at + 2 * tile_count + k], live[0, slot, k]) != 0
        take, to = places[1 - out_axis], jnp.where(present, places[out_axis], spare)
        block = source[pl.ds(pl.multiple_of(take * size, size), size), :]
        rows = pl.ds(pl.multiple_of(to * size, size), size)
        total[rows, :] += dot(tiles[order, k], block, ((1 - out_axis,), (0,)))


def forward(swap, coords, live, note, tiles, far, near, panel, keep, send, source, total):
    rows = panel.shape[0]
    total[...] = jnp.zeros_like(total)
    place_tiles(swap, 0, 0, coords, live, note, tiles, far, total)
    is_local = near_is_local(swap, lax.axis_index("blk"), lax.axis_index("rep"))

    @pl.when(is_local)
    def _():
        source[...] = panel[...]

    @pl.when(jnp.logical_not(is_local))
    def _():
        source[...] = near[...]

    place_tiles(swap, 1, 0, coords, live, note, tiles, source, total)
    core = lax.rem(lax.axis_index("rep"), 2)
    share = rows // 4
    for h in range(2):
        mine = pl.ds(pl.multiple_of((2 * h + core) * share, share), share)
        other = pl.ds(pl.multiple_of((2 * h + 1 - core) * share, share), share)
        keep[h * share : (h + 1) * share, :] = total[mine, :]
        send[h * share : (h + 1) * share, :] = total[other, :].astype(BF16)


def picked_slot(tiles, picked, sem):
    rep = lax.axis_index("rep")

    @pl.when(swaps_slot(True, lax.axis_index("blk"), rep))
    def _():
        copy = pltpu.make_async_copy(tiles.at[0, 1 - lax.div(rep, 2)], picked, sem)
        copy.start()
        copy.wait()


def prepare(
    swap, tiles, features, *rest,
):
    moved = rest[:-3]
    kept_tiles, panel, sems = rest[-3:]
    rep = lax.axis_index("rep")
    copies = [pltpu.make_async_copy(features, panel, sems.at[4])]
    for copy in copies:
        copy.start()

    tile_copies = []
    for order in range(2):
        is_moved, slot = slot_of(swap, order, rep, lax.axis_index("blk"))
        place = kept_tiles.at[order]
        here = pltpu.make_async_copy(tiles.at[0, slot], place, sems.at[len(tile_copies)])
        tile_copies.append((jnp.logical_not(is_moved), here))
        if moved:
            come = pltpu.make_async_copy(moved[0], place, sems.at[len(tile_copies)])
            tile_copies.append((is_moved, come))
    for is_needed, copy in tile_copies:
        pl.when(is_needed)(copy.start)
    for copy in copies:
        copy.wait()
    for is_needed, copy in tile_copies:
        pl.when(is_needed)(copy.wait)


def row_terms(panel, cot_own, deg_own, w_self, cot_far, deg_far, self_term, cot, inv_root):
    rep = lax.axis_index("rep")
    core, plane = lax.rem(rep, 2), lax.div(rep, 2)
    share = cot_own.shape[0]
    near = pl.ds(pl.multiple_of(plane * share, share), share)
    away = pl.ds(pl.multiple_of((1 - plane) * share, share), share)
    cot[near, :] = cot_own[...]
    cot[away, :] = cot_far[...]
    width = inv_root.shape[1]
    for where, deg in ((near, deg_own[...]), (away, deg_far[:1, :])):
        inv_root[where, :] = jnp.transpose(jnp.broadcast_to(1.0 / jnp.sqrt(deg.astype(F32)), (width, share)))
    for h in range(2):
        rows = panel[pl.ds(pl.multiple_of((2 * h + core) * share, share), share), :]
        self_term[h * share : (h + 1) * share, :] = dot(rows, w_self[...], ((1,), (0,)))


def middle(chip_sum, far_sum, inv_root, self_term, cot, panel, w_self, w_neigh, hidden, own_term, message, kept_grad, grads):
    rep = lax.axis_index("rep")
    core, plane = lax.rem(rep, 2), lax.div(rep, 2)
    half, share = chip_sum.shape[0], hidden.shape[0]
    inv = inv_root[...]
    aggregate = ((chip_sum[...] + far_sum[...].astype(F32)) * inv).astype(BF16)
    preact = self_term[...] + dot(aggregate, w_neigh[...], ((1,), (0,)))
    sig = jax.nn.sigmoid(preact)
    slope = sig * (1.0 + preact * (1.0 - sig))
    grad = (cot[...].astype(F32) * slope).astype(BF16)
    message[:half, :] = (dot(grad, w_neigh[...], ((1,), (1,))) * inv).astype(BF16)
    own = [panel[pl.ds(pl.multiple_of((2 * h + core) * share, share), share), :] for h in range(2)]
    left = jnp.where(plane == 0, jnp.concatenate(own).astype(F32), aggregate.astype(F32)).astype(BF16)
    grads[...] = dot(left, grad, ((0,), (0,)))
    rows = kept_grad.shape[0]
    kept_grad[...] = grads[pl.ds(pl.multiple_of(core * rows, rows), rows), :]
    message[half:, :] = grads[pl.ds(pl.multiple_of((1 - core) * rows, rows), rows), :].astype(BF16)
    value = (preact * sig).astype(BF16)
    term = dot(grad, w_self[...], ((1,), (1,)))

    @pl.when(plane == 0)
    def _():
        hidden[...] = value[:share]
        own_term[...] = term[:share]

    @pl.when(plane != 0)
    def _():
        hidden[...] = value[share:]
        own_term[...] = term[share:]


def backward(swap, coords, live, note, tiles, own, other, far_cross, far_same, near_first, near_last, source, total):
    rep = lax.axis_index("rep")
    core, plane = lax.rem(rep, 2), lax.div(rep, 2)
    share = source.shape[0] // 4
    for h in range(2):
        part = slice(h * share, (h + 1) * share)
        source[pl.ds(pl.multiple_of((2 * h + core) * share, share), share), :] = own[part, :]
        source[pl.ds(pl.multiple_of((2 * h + 1 - core) * share, share), share), :] = other[part, :]
    half = 2 * share
    same_first = home_first(swap, lax.axis_index("blk"), rep)
    to_plane = jnp.where(same_first, plane, 1 - plane)
    for slot, outs in enumerate(((far_cross, far_same), (near_first, near_last))):
        total[...] = jnp.zeros_like(total)
        place_tiles(swap, slot, 1, coords, live, note, tiles, source, total)
        first = 1 - plane if slot == 0 else to_plane
        for out, which in zip(outs, (first, 1 - first)):
            out[...] = total[pl.ds(pl.multiple_of(which * half, half), half), :].astype(BF16)


def swaps_slot(swap, part, rep):
    return (part % 2 == 0) & (rep % 2 == 0) & swap


def near_is_local(swap, part, rep):
    return rep == (2 * (part % 2) if swap else 2)


def home_first(swap, part, rep):
    return (rep == 2 * (part % 2)) & swap


def kernel_call(kernel, name, outs, args, scratch=(), in_specs=None, out_specs=None):
    return pl.pallas_call(
        kernel,
        out_shape=[jax.ShapeDtypeStruct(*out) for out in outs],
        in_specs=in_specs or [VMEM] * len(args),
        out_specs=out_specs or [VMEM] * len(outs),
        scratch_shapes=scratch,
        compiler_params=pltpu.CompilerParams(vmem_limit_bytes=8 * 2**20),
        name=name,
    )(*args)


def on_device(tile_vals, tile_coords, tile_live, features, degree, w_self, w_neigh, cotangent):
    part_total = lax.axis_size("blk")
    rep_count = lax.axis_size("rep")
    rep = lax.axis_index("rep")
    core, plane = rep % 2, rep // 2
    slots, tile_size = tile_vals.shape[1], tile_vals.shape[3]
    half_span = slots * rep_count // 2
    rows, dim = features.shape
    half, share = rows // 2, rows // rep_count

    swap = part_total == slots * rep_count

    def far(part, r):
        if swap and r == 2 and part % 2 == 0:
            return 1 - half_span
        return slots * r + r // 2 - half_span

    def near(part, r):
        if swap and r in (0, 2) and part % 2 == 0:
            return 0 if r == 0 else 1
        return slots * r + 1 - r // 2 - half_span

    def flip_core(value):
        return exchange(value, lambda b, r: (b, r ^ 1))

    def flip_plane(value):
        return exchange(value, lambda b, r: (b, r ^ 2))

    def fetch(shift):
        pairs = []
        for part in range(part_total):
            for r in range(rep_count):
                if shift(part, r):
                    pairs.append((((part + shift(part, r)) % part_total) * rep_count + r, part * rep_count + r))
        return lax.ppermute(features, BOTH, pairs)

    panel_far, panel_near = fetch(far), fetch(near)

    def note_of(slot):
        parts = [degree, tile_coords[0, slot].reshape(-1), tile_live[0, slot]]
        parts.append(jnp.zeros((2 * share - sum(p.size for p in parts),), jnp.int32))
        return jnp.concatenate(parts)

    far_note = flip_plane(jnp.where(plane == 0, note_of(1), note_of(0)))
    cot_far = flip_plane(cotangent)
    moved = []
    if swap:
        pairs = []
        for part in range(0, part_total, 2):
            pairs += [(part * rep_count, part * rep_count + 2), (part * rep_count + 2, part * rep_count)]
        picked = kernel_call(
            picked_slot, "picked_slot", [(tile_vals.shape[2:], BF16)], [pltpu.with_memory_space_constraint(tile_vals, pltpu.HBM)],
            [pltpu.SemaphoreType.DMA], [pl.BlockSpec(memory_space=pltpu.HBM)],
        )[0]
        moved.append(lax.ppermute(picked, BOTH, pairs))
    wide = (half, dim)
    raw = [pltpu.with_memory_space_constraint(a, pltpu.HBM) for a in (tile_vals, features)]
    tiles, panel = kernel_call(
        functools.partial(prepare, swap), "prepare", [(tile_vals.shape[1:], BF16), ((rows, dim), BF16)], raw + moved,
        [pltpu.SemaphoreType.DMA((5,))],
        [pl.BlockSpec(memory_space=pltpu.HBM)] * 2 + [pl.BlockSpec(memory_space=pl.ANY)] * len(moved),
    )
    far_note, cot_far, panel = lax.optimization_barrier((far_note, cot_far, panel))
    self_term, cot, inv_root = kernel_call(
        row_terms, "row_terms", [(wide, F32), (wide, BF16), (wide, F32)],
        [panel, cotangent, degree.reshape(1, share), w_self, cot_far, far_note.reshape(2, share)],
    )

    source, total = pltpu.VMEM((rows, dim), BF16), pltpu.VMEM((rows + tile_size, dim), F32)
    scalars = [tile_coords.transpose(0, 1, 3, 2), tile_live, far_note]
    keep, send = kernel_call(
        functools.partial(forward, swap), "forward", [(wide, F32), (wide, BF16)], scalars + [tiles, panel_far, panel_near, panel],
        [source, total], [SMEM] * 3 + [VMEM] * 4,
    )
    chip_sum = keep + flip_core(send).astype(F32)
    far_sum = flip_plane(chip_sum.astype(BF16))

    grad_rows = dim // 2
    hidden, own_term, message, kept_grad = kernel_call(
        middle,
        "middle",
        [((share, dim), BF16), ((share, dim), F32), ((half + grad_rows, dim), BF16), ((grad_rows, dim), F32)],
        [chip_sum, far_sum, inv_root, self_term, cot, panel, w_self, w_neigh],
        [pltpu.VMEM((dim, dim), F32)],
    )
    other = flip_core(message)
    sends = kernel_call(
        functools.partial(backward, swap), "backward", [(wide, BF16)] * 4, scalars + [tiles, message, other], [source, total],
        [SMEM] * 3 + [VMEM] * 3,
    )

    def others(value, bit, rep_bit=0):
        return exchange(value, lambda b, r: (b ^ bit, r ^ rep_bit))

    def added(one, two):
        return (one.astype(F32) + two.astype(F32)).astype(BF16)

    def tied(value, *after):
        return lax.optimization_barrier((value,) + after)[0]

    sends = list(sends)
    rounded = (kept_grad + other[half:].astype(F32)).astype(BF16)
    top = part_total.bit_length() - 2
    def near_first(part, r, flip):
        return (part + near(part, r), r if bool(home_first(swap, part, r)) != flip else r ^ 2)

    arrived = [
        exchange(sends[0], lambda b, r: (b + far(b, r), r ^ 2)),
        exchange(sends[1], lambda b, r: (b + far(b, r), r)),
        exchange(sends[2], lambda b, r: near_first(b, r, False)),
        exchange(sends[3], lambda b, r: near_first(b, r, True)),
    ]

    rounded = added(rounded, tied(others(rounded, 1 << top), sends[0]))
    for i in range(top - 1, 1, -1):
        rounded = added(rounded, others(rounded, 1 << i))
    rounded = added(rounded, tied(others(rounded, 2), arrived[0]))
    rounded = added(rounded, tied(others(rounded, 1), arrived[1], arrived[2]))
    twin = flip_plane(rounded)
    by_plane = jnp.where(plane == 0, jnp.stack([rounded, twin]), jnp.stack([twin, rounded]))
    twin = flip_core(by_plane)
    by_core = jnp.where(core == 0, jnp.stack([by_plane, twin], 1), jnp.stack([twin, by_plane], 1))
    grad_scale = 1.0 / math.sqrt(rows * part_total)
    totals = by_core.reshape(2, dim, dim).astype(F32) * grad_scale

    neighbour = sum(a.astype(F32) for a in arrived).reshape(2, share, dim)
    twin = flip_core(lax.dynamic_index_in_dim(neighbour, 1 - core, 0, keepdims=False).astype(BF16))
    neighbour = lax.dynamic_index_in_dim(neighbour, core, 0, keepdims=False) + twin.astype(F32)
    grad_features = (own_term + neighbour).astype(BF16)
    return (hidden, grad_features, totals[0], totals[1])


def solution(mesh):
    return jax.shard_map(
        on_device,
        mesh=mesh,
        in_specs=(
            P("blk", "rep", None, None, None),
            P("blk", "rep", None, None),
            P("blk", "rep", None),
            P("blk", None),
            P(("blk", "rep")),
            P(),
            P(),
            P(("blk", "rep"), None),
        ),
        out_specs=(P(("blk", "rep"), None), P(("blk", "rep"), None), P(), P()),
        check_vma=False,
    )
```
